128 devices in a mesh: group: 4 (over z_hi, core), tensor: 32 (over z_lo, y, x).
Axes of the slice: x: 4, y: 4, z: 4 (z_hi: 2, z_lo: 2; z = z_hi * 2 + z_lo), core: 2. Of those that a mesh axis runs over, the one named last changes fastest.
Arguments:
- hidden: bfloat16 [1024, 2, 8192], P('group', None, 'tensor'), may hold values from -6 to 6
- query_weight: bfloat16 [8192, 8192], P(None, 'tensor'), may hold values from -0.0625 to 0.0625
- key_weight: bfloat16 [8192, 1024], P(None, 'tensor'), may hold values from -0.0625 to 0.0625
- value_weight: bfloat16 [8192, 1024], P(None, 'tensor'), may hold values from -0.0625 to 0.0625
- output_weight: bfloat16 [8192, 8192], P('tensor'), may hold values from -0.25 to 0.25
- adapter_down_maps: bfloat16 [32, 8192, 128], P(None, 'tensor'), may hold values from -0.0625 to 0.0625
- adapter_up_query: bfloat16 [32, 64, 8192], P(None, None, 'tensor'), may hold values from -0.75 to 0.75
- adapter_up_value: bfloat16 [32, 64, 1024], P(None, None, 'tensor'), may hold values from -0.75 to 0.75
- key_value_pages: bfloat16 [4096, 64, 2048], P(('group', 'tensor')), may hold values from -1300 to 1300
- row_adapter_index: int32 [1024], P('group'), may hold values from 0 to 31
- row_rank_bucket: int32 [1024], P('group'), may hold values from 16 to 64, as said below
- lengths: int32 [1024], replicated, may hold values from 1 to 256, as said below
- row_page_index: int32 [1024, 4], replicated, may hold values from 0 to 4095, as said below
Outputs:
- output: bfloat16 [1024, 2, 8192], P('group', None, 'tensor')
The draws below stay inside these ranges and needn't reach their ends.
Inputs may be any that keep to these rules, and one draw needn't show every extreme that they name: `row_page_index`: every page id is used by exactly one (row, slot). Device d = r // 8 numbers the devices group after group. A row is either local, with all its pages in the ids d * 8 * 4 to (d + 1) * 8 * 4 - 1 of its own device, or resumed, with all of them in the ids of the device with the same tensor index in the next group, cyclically. The rows of each device, 8 in an aligned block, hold exactly 4 resumed rows. `lengths`: the rows of each device include one of length 256. `row_rank_bucket`: one of 64, 32 and 16.
All inputs are finite; a program needn't handle non-finite values.
Results may differ from the reference program's by a relative error of at most 0.03.
Values may be sent and summed in bfloat16 or wider, within the bound.
A program may use at most 192 MiB of HBM per device.

```python
import math
import jax
import jax.numpy as jnp
import numpy as np
from jax import lax

MODEL_WIDTH = 8192
QUERY_HEADS = 64
KEY_VALUE_HEADS = 8
HEAD_SIZE = 128
RANK_LIMIT = 64
ADAPTER_COUNT = 32
P_SIZE = 64
MAXP = 4
ROWS_DEV = 8
STEPS = 2
RES = 4
GROUP_ROWS = 256
ROWS = 1024
CTX = 256
PAGES = 4096
N_TENSOR = 32


def resumed_flags(key):
    device_count = ROWS // ROWS_DEV
    keys_all = jax.random.split(jax.random.fold_in(key, 11), device_count)
    orders = jax.vmap(lambda one_key: jax.random.permutation(one_key, ROWS_DEV))(keys_all)
    ranks = jnp.argsort(orders, axis=1)
    return (ranks < RES).astype(jnp.int32).reshape(ROWS)


def draw_row_page_index(key, part):
    flags = resumed_flags(key).reshape(ROWS // ROWS_DEV, ROWS_DEV)
    key = jax.random.fold_in(key, 3)
    device_count = ROWS // ROWS_DEV
    group_width = GROUP_ROWS // ROWS_DEV
    before_res = jnp.cumsum(flags, axis=1) - flags
    before_own = jnp.cumsum(1 - flags, axis=1) - (1 - flags)
    slot_ids = jnp.arange(MAXP, dtype=jnp.int32)
    own_index = before_own[:, :, None] * MAXP + slot_ids
    res_index = (ROWS_DEV - RES) * MAXP + before_res[:, :, None] * MAXP + slot_ids
    index_all = jnp.where(flags[:, :, None] == 1, res_index, own_index)
    device_ids = jnp.arange(device_count, dtype=jnp.int32)
    owner = jnp.where(flags == 1, (device_ids[:, None] + group_width) % device_count, device_ids[:, None])
    per_device = ROWS_DEV * MAXP
    keys_all = jax.random.split(key, device_count)
    shuffles = jax.vmap(lambda one_key: jax.random.permutation(one_key, per_device))(keys_all)
    local_ids = shuffles[owner[:, :, None], index_all]
    return (owner[:, :, None] * per_device + local_ids).reshape(ROWS, MAXP).astype(jnp.int32)


def draw_lengths(key, part):
    key = jax.random.fold_in(key, 5)
    first_key, second_key = jax.random.split(key)
    device_count = ROWS // ROWS_DEV
    base_len = jax.random.randint(first_key, (device_count, ROWS_DEV), 1, CTX + 1)
    chosen = jax.random.randint(second_key, (device_count,), 0, ROWS_DEV)
    longest = jnp.arange(ROWS_DEV)[None, :] == chosen[:, None]
    return jnp.where(longest, CTX, base_len).reshape(ROWS).astype(jnp.int32)


def draw_row_rank_bucket(key, part):
    key = jax.random.fold_in(key, 7)
    first_key, second_key, third_key = jax.random.split(key, 3)
    table = jnp.array([RANK_LIMIT, RANK_LIMIT // 2, RANK_LIMIT // 4], dtype=jnp.int32)
    bucket = table[jax.random.randint(first_key, (ROWS,), 0, 3)]
    spot_high = jax.random.randint(second_key, (), 0, ROWS)
    spot_low = (spot_high + 1 + jax.random.randint(third_key, (), 0, ROWS - 1)) % ROWS
    row_ids = jnp.arange(ROWS)
    bucket = jnp.where(row_ids == spot_high, RANK_LIMIT, bucket)
    bucket = jnp.where(row_ids == spot_low, RANK_LIMIT // 4, bucket)
    return bucket.astype(jnp.int32)


def draw_key_value_pages(key, part):
    key = jax.random.fold_in(key, 13)
    first_key = jax.random.fold_in(key, 0)
    shape = (PAGES, P_SIZE, 2 * KEY_VALUE_HEADS * HEAD_SIZE)
    return jax.random.truncated_normal(first_key, -4.0, 4.0, shape, jnp.float32).astype(jnp.bfloat16)


def place_ends(values, own_key, smallest, largest):
    place = [jax.random.randint(jax.random.fold_in(own_key, axis), (), 0, length) for axis, length in enumerate(values.shape)]
    widest = values.shape.index(max(values.shape))
    beside = place[:widest] + [(place[widest] + 1) % values.shape[widest]] + place[widest + 1:]
    return values.at[tuple(place)].set(smallest).at[tuple(beside)].set(largest)


def steps_of(key, extent, shards, low, high):
    def one(dim, parts):
        steps = jax.random.uniform(jax.random.fold_in(jax.random.fold_in(key, 6), dim), (parts,), jnp.float32, low / len(shards), high / len(shards))
        return jnp.repeat(jnp.exp(steps), extent[dim] // parts).reshape((-1,) + (1,) * (len(extent) - dim - 1))

    gain = one(*shards[0])
    for cut in shards[1:]:
        gain = gain * one(*cut)
    return gain


def rank_bounds(count, skew):
    loads = [(1 << 20) // math.isqrt(grade ** skew) + 1 for grade in range(1, count + 1)]
    width = 1 + sum(loads) // (1 << 30)
    return np.cumsum(np.array([max(1, weight // width) for weight in loads]))


def ranked(own_key, shape, count, skew):
    table = rank_bounds(count, skew)
    ticket = jax.random.randint(jax.random.fold_in(own_key, 1), shape, 0, int(table[count - 1]))
    rank = jnp.searchsorted(jnp.asarray(table, jnp.int32), ticket, side="right")
    return jax.random.permutation(jax.random.fold_in(own_key, 2), count)[rank].astype(jnp.int32)


def bell_draw(stream_key, shape, scale, reach, cuts=(), kind=jnp.bfloat16):
    values = jax.random.normal(stream_key, shape, jnp.float32) * scale
    if len(cuts) > 0:
        values = steps_of(stream_key, shape, cuts, -0.22, 0.18) * values
    return jnp.clip(values, min=-reach, max=reach).astype(kind)


def setup_inputs(seed: int = 0) -> dict:
    seeds = jax.random.split(jax.random.key(seed), 14)
    hidden = bell_draw(seeds[0], (ROWS, STEPS, MODEL_WIDTH), 1.0, 6.0, ((0, 4), (2, 32)))
    query_weight = bell_draw(seeds[1], (MODEL_WIDTH, QUERY_HEADS * HEAD_SIZE), MODEL_WIDTH ** -0.5, 0.0625, ((1, 32),))
    key_weight = bell_draw(seeds[2], (MODEL_WIDTH, KEY_VALUE_HEADS * HEAD_SIZE), MODEL_WIDTH ** -0.5, 0.0625, ((1, 32),))
    value_weight = bell_draw(seeds[3], (MODEL_WIDTH, KEY_VALUE_HEADS * HEAD_SIZE), MODEL_WIDTH ** -0.5, 0.0625, ((1, 32),))
    output_weight = bell_draw(seeds[4], (QUERY_HEADS * HEAD_SIZE, MODEL_WIDTH), (QUERY_HEADS * HEAD_SIZE // 16) ** -0.5, 0.25, ((0, 32),))
    adapter_down_maps = bell_draw(seeds[5], (ADAPTER_COUNT, MODEL_WIDTH, 2 * RANK_LIMIT), MODEL_WIDTH ** -0.5, 0.0625, ((1, 32),))
    adapter_up_query = bell_draw(seeds[6], (ADAPTER_COUNT, RANK_LIMIT, QUERY_HEADS * HEAD_SIZE), RANK_LIMIT ** -0.5, 0.75, ((2, 32),))
    adapter_up_value = bell_draw(seeds[7], (ADAPTER_COUNT, RANK_LIMIT, KEY_VALUE_HEADS * HEAD_SIZE), RANK_LIMIT ** -0.5, 0.75, ((2, 32),))
    key_value_pages = draw_key_value_pages(jax.random.fold_in(seeds[13], 71), 0)
    row_adapter_index = place_ends(ranked(seeds[9], (ROWS,), ADAPTER_COUNT, 2), jax.random.fold_in(seeds[9], 3), 0, ADAPTER_COUNT - 1).astype(jnp.int32)
    row_rank_bucket = draw_row_rank_bucket(jax.random.fold_in(seeds[13], 71), 0)
    lengths = draw_lengths(jax.random.fold_in(seeds[13], 71), 0)
    row_page_index = draw_row_page_index(jax.random.fold_in(seeds[13], 71), 0)
    return {"hidden": hidden, "query_weight": query_weight, "key_weight": key_weight, "value_weight": value_weight, "output_weight": output_weight, "adapter_down_maps": adapter_down_maps, "adapter_up_query": adapter_up_query, "adapter_up_value": adapter_up_value, "key_value_pages": key_value_pages, "row_adapter_index": row_adapter_index, "row_rank_bucket": row_rank_bucket, "lengths": lengths, "row_page_index": row_page_index}


ROPE_BASE = 500000.0


def rotate(values, positions):
    half_dim = values.shape[-1] // 2
    inverse_freq = jnp.exp(-math.log(ROPE_BASE) * jnp.arange(half_dim, dtype=jnp.float32) / half_dim)
    angles = positions.astype(jnp.float32)[..., None, None] * inverse_freq
    cos_part = jnp.cos(angles)
    sin_part = jnp.sin(angles)
    first_half = values[..., :half_dim]
    second_half = values[..., half_dim:]
    return jnp.concatenate([first_half * cos_part - second_half * sin_part, second_half * cos_part + first_half * sin_part], axis=-1)


def attend(query_rows, kv_cache, keys_new, fresh_value_rows, row_lengths):
    batch_rows = kv_cache.shape[0]
    ctx_len = kv_cache.shape[1]
    key_block = jnp.concatenate([kv_cache[:, :, :KEY_VALUE_HEADS * HEAD_SIZE], keys_new], axis=1).reshape(batch_rows, ctx_len + STEPS, KEY_VALUE_HEADS, HEAD_SIZE)
    value_block = jnp.concatenate([kv_cache[:, :, KEY_VALUE_HEADS * HEAD_SIZE:], fresh_value_rows], axis=1).reshape(batch_rows, ctx_len + STEPS, KEY_VALUE_HEADS, HEAD_SIZE)
    grouped = query_rows.reshape(batch_rows, STEPS, KEY_VALUE_HEADS, QUERY_HEADS // KEY_VALUE_HEADS, HEAD_SIZE)
    scores = jnp.einsum('rsngd,rtnd->rsngt', grouped.astype(jnp.float32), key_block.astype(jnp.float32)) * (HEAD_SIZE ** -0.5)
    slot_pos = jnp.arange(ctx_len + STEPS)
    step_pos = jnp.arange(STEPS)
    in_cache = slot_pos[None, None, :] < row_lengths[:, None, None]
    in_steps = (slot_pos[None, :] - ctx_len) <= step_pos[:, None]
    usable = jnp.where(slot_pos[None, None, :] < ctx_len, in_cache, in_steps[None, :, :])[:, :, None, None, :]
    peak_score = jnp.max(jnp.where(usable, scores, -jnp.inf), axis=-1, keepdims=True)
    weights_raw = jnp.where(usable, jnp.exp(scores - peak_score), 0.0)
    totals = jnp.sum(weights_raw, axis=-1)
    probs = lax.optimization_barrier(weights_raw.astype(jnp.bfloat16))
    mixture = jnp.einsum('rsngt,rtnd->rsngd', probs.astype(jnp.float32), value_block.astype(jnp.float32))
    return (mixture / totals[..., None]).astype(jnp.bfloat16).reshape(batch_rows, STEPS, QUERY_HEADS * HEAD_SIZE)


def reference(hidden, query_weight, key_weight, value_weight, output_weight, adapter_down_maps, adapter_up_query, adapter_up_value, key_value_pages, row_adapter_index, row_rank_bucket, lengths, row_page_index):
    rows_all = hidden.shape[0]
    rank_slice_width = MODEL_WIDTH // N_TENSOR
    onehot = (row_adapter_index[:, None] == jnp.arange(ADAPTER_COUNT)[None, :]).astype(jnp.float32)

    def add_low(total, page_block_index):
        slice_x = lax.dynamic_slice_in_dim(hidden, page_block_index * rank_slice_width, rank_slice_width, 2).astype(jnp.float32)
        down_map_slice = lax.dynamic_slice_in_dim(adapter_down_maps, page_block_index * rank_slice_width, rank_slice_width, 1).astype(jnp.float32)
        partial_value = jnp.einsum('rsd,adk->rsak', slice_x, down_map_slice)
        chosen = jnp.einsum('rsak,ra->rsk', partial_value, onehot)
        rounded = lax.optimization_barrier(chosen.astype(jnp.bfloat16))
        return total + rounded.astype(jnp.float32), None

    lowrank, _ = lax.scan(add_low, jnp.zeros((rows_all, STEPS, 2 * RANK_LIMIT), jnp.float32), jnp.arange(N_TENSOR, dtype=jnp.int32))
    column = jnp.arange(2 * RANK_LIMIT) % RANK_LIMIT
    bucket = row_rank_bucket[:, None, None]
    scaled = jnp.where(column[None, None, :] < bucket, lowrank * (0.5 * RANK_LIMIT) / bucket.astype(jnp.float32), 0.0).astype(jnp.bfloat16)
    mask_rows = onehot.astype(jnp.bfloat16)[:, None, :, None]
    lifted_query = (mask_rows * scaled[:, :, None, :RANK_LIMIT]).reshape(rows_all * STEPS, ADAPTER_COUNT * RANK_LIMIT)
    lifted_value = (mask_rows * scaled[:, :, None, RANK_LIMIT:]).reshape(rows_all * STEPS, ADAPTER_COUNT * RANK_LIMIT)
    flat_layout = hidden.reshape(rows_all * STEPS, MODEL_WIDTH)
    query_rows = jnp.dot(flat_layout, query_weight, preferred_element_type=jnp.float32) + jnp.dot(lifted_query, adapter_up_query.reshape(ADAPTER_COUNT * RANK_LIMIT, QUERY_HEADS * HEAD_SIZE), preferred_element_type=jnp.float32)
    keys_new = jnp.dot(flat_layout, key_weight, preferred_element_type=jnp.float32)
    fresh_value_rows = jnp.dot(flat_layout, value_weight, preferred_element_type=jnp.float32) + jnp.dot(lifted_value, adapter_up_value.reshape(ADAPTER_COUNT * RANK_LIMIT, KEY_VALUE_HEADS * HEAD_SIZE), preferred_element_type=jnp.float32)
    query_rows = lax.optimization_barrier(query_rows.astype(jnp.bfloat16)).reshape(rows_all, STEPS, QUERY_HEADS, HEAD_SIZE)
    keys_new = lax.optimization_barrier(keys_new.astype(jnp.bfloat16)).reshape(rows_all, STEPS, KEY_VALUE_HEADS, HEAD_SIZE)
    fresh_value_rows = fresh_value_rows.astype(jnp.bfloat16).reshape(rows_all, STEPS, KEY_VALUE_HEADS * HEAD_SIZE)
    positions = lengths[:, None] + jnp.arange(STEPS, dtype=jnp.int32)[None, :]
    rotated_queries = rotate(query_rows.astype(jnp.float32), positions).astype(jnp.bfloat16).reshape(rows_all, STEPS, QUERY_HEADS * HEAD_SIZE)
    rotated_keys = rotate(keys_new.astype(jnp.float32), positions).astype(jnp.bfloat16).reshape(rows_all, STEPS, KEY_VALUE_HEADS * HEAD_SIZE)

    def one_row(items):
        row_query, row_keys, row_values, row_pages, row_length = items
        kv_cache = key_value_pages[row_pages].reshape(1, MAXP * P_SIZE, 2 * KEY_VALUE_HEADS * HEAD_SIZE)
        return attend(row_query[None], kv_cache, row_keys[None], row_values[None], row_length[None])[0]

    attended = lax.map(one_row, (rotated_queries, rotated_keys, fresh_value_rows, row_page_index, lengths))
    head_width = QUERY_HEADS * HEAD_SIZE // N_TENSOR

    def add_out(total, page_block_index):
        block = lax.dynamic_slice_in_dim(attended, page_block_index * head_width, head_width, 2).reshape(rows_all * STEPS, head_width)
        weights = lax.dynamic_slice_in_dim(output_weight, page_block_index * head_width, head_width, 0)
        part_out = lax.optimization_barrier(jnp.dot(block, weights, preferred_element_type=jnp.float32).astype(jnp.bfloat16))
        return total + part_out.astype(jnp.float32), None

    summed, _ = lax.scan(add_out, jnp.zeros((rows_all * STEPS, MODEL_WIDTH), jnp.float32), jnp.arange(N_TENSOR, dtype=jnp.int32))
    return summed.reshape(rows_all, STEPS, MODEL_WIDTH).astype(jnp.bfloat16)
```

```python
import functools
import math

import jax
import jax.numpy as jnp
from jax import lax
from jax.experimental import pallas as pl
from jax.experimental.pallas import tpu as pltpu
from jax.sharding import PartitionSpec as P

QUERY_HEADS = 64
KEY_VALUE_HEADS = 8
HEAD_SIZE = 128
RANK_LIMIT = 64
ADAPTERS = 32
STEPS = 2
RES = 4
ROWS_DEV = 8
TOKENS = 512
POOL = 32
ROPE_BASE = 500000.0
MESH = pl.DeviceIdType.MESH
F32 = jnp.float32
BF16 = jnp.bfloat16


def dot(a, b):
    return jnp.dot(a, b, preferred_element_type=F32)


def dot_nt(a, b):
    return lax.dot_general(a, b, (((1,), (1,)), ((), ())), preferred_element_type=F32)


def dot_tn(a, b):
    return lax.dot_general(a, b, (((0,), (0,)), ((), ())), preferred_element_type=F32)


def remote(src, dst, send, recv, device):
    return pltpu.make_async_remote_copy(
        src_ref=src, dst_ref=dst, send_sem=send, recv_sem=recv,
        device_id=device, device_id_type=MESH,
    )


def kernel(
    hid, meta, pos_row, pos_col, cos_t, sin_t, lens, pids,
    qw, kt, vt, ow, down, upq, upv, pool,
    out,
    hb, wq, wqp, kvt, wo, pages, dn, uq, uv,
    acc, metap, lowsend, lowrecv, scown, screcv, lift, liftv,
    send1, recv1, qs, kvs, knf, vnf, att, send2, recv2, lhs,
    sb, sf, rh, rf, ta, rah, raf,
    loc, ags, agr, wxs, wxr, fws, fwr, lows, lowr, scs, scr, s1s, s1r, s2s, s2r, rss, rsr,
):
    g = lax.axis_index("group")
    t = lax.axis_index("tensor")
    core = g % 2
    z = t // 16
    y = (t // 4) % 4
    x = t % 4
    zp = 1 - z
    tp = zp * 16 + y * 4 + x
    g2 = (g + 2) % 4
    gs = g + 1 - 2 * core

    def near(along_b, d):
        on_x = (1 - core) * (1 - along_b) + core * along_b
        on_y = 1 - on_x
        xx = (x + 4 + d * on_x) % 4
        yy = (y + 4 + d * on_y) % 4
        return (g, z * 16 + yy * 4 + xx)

    def slice_index(oa, ob):
        dx = oa * (1 - core) + ob * core
        dy = oa * core + ob * (1 - core)
        return ((y + dy) % 4) * 4 + (x + dx) % 4

    half = z * 4096
    local = [
        (qw.at[pl.ds(pl.multiple_of(half, 4096), 4096)], wq),
        (kt.at[:, pl.ds(pl.multiple_of(half, 4096), 4096)], kvt.at[pl.ds(pl.multiple_of(z * 64, 32), 32)]),
        (vt.at[:, pl.ds(pl.multiple_of(half, 4096), 4096)], kvt.at[pl.ds(pl.multiple_of(z * 64 + 32, 32), 32)]),
        (ow.at[:, pl.ds(pl.multiple_of(half, 4096), 4096)], wo.at[z]),
        (down, dn),
        (upq, uq),
        (upv, uv),
        (pool, pages),
    ]
    local = [pltpu.make_async_copy(s, d, loc.at[i]) for i, (s, d) in enumerate(local)]
    local[4].start()
    local[0].start()

    perm = (lax.broadcasted_iota(jnp.int32, (TOKENS, TOKENS), 0) == pos_row[...]).astype(BF16)
    hb[0, 0] = dot(perm, hid[...]).astype(BF16)

    def ag_copy(row, kind):
        along_b = 1 if row else 0
        oa = row - 1

        def at(o, rows=None):
            ref = hb.at[oa, o] if along_b else hb.at[o, 0]
            return ref if rows is None else ref.at[pl.ds(rows, 256)]

        if kind == 0:
            src, dst, d = at(0), at(1), -1
        elif kind == 1:
            src, dst, d = at(0), at(3), 1
        elif kind == 2:
            src, dst, d = at(1, 0), at(2, 0), -1
        else:
            src, dst, d = at(3, 256), at(2, 256), 1
        return remote(src, dst, ags.at[row, kind], agr.at[row, kind], near(along_b, d))

    ag = [[ag_copy(row, kind) for kind in range(4)] for row in range(5)]
    for row in (0, 1):
        for kind in (0, 1):
            ag[row][kind].start()

    def wx_pieces(zq, q, zd):
        c0 = pl.multiple_of(zd * 4096 + q * 1024, 1024)
        d0 = pl.multiple_of(q * 1024, 1024)
        r0 = pl.multiple_of(q * 64, 64)
        return [
            (qw.at[pl.ds(c0, 1024)], wqp.at[pl.ds(d0, 1024)]),
            (kt.at[:, pl.ds(c0, 1024)], kvt.at[pl.ds(pl.multiple_of(zq * 64, 32), 32), pl.ds(d0, 1024)]),
            (vt.at[:, pl.ds(c0, 1024)], kvt.at[pl.ds(pl.multiple_of(zq * 64 + 32, 32), 32), pl.ds(d0, 1024)]),
            (ow.at[pl.ds(r0, 64), pl.ds(pl.multiple_of(zd * 4096, 4096), 4096)], wo.at[zq, pl.ds(r0, 64)]),
        ]

    def wx_copies(i):
        s, d = wx_pieces(z, g, zp)[i]
        return [remote(s, d, wxs.at[i, j], wxr.at[i, j], (gd, tp)) for j, gd in enumerate((g, g2))]

    def wx_arrivals(i):
        res = []
        for j, q in enumerate((g, g2)):
            s, d = wx_pieces(zp, q, z)[i]
            res.append(remote(s, d, wxs.at[i, j], wxr.at[i, j], (g, tp)))
        return res

    def fw_copies(i):
        res = []
        for j, q in enumerate((g, g2)):
            _, d = wx_pieces(zp, q, z)[i]
            res.append(remote(d, d, fws.at[i, j], fwr.at[i, j], (gs, t)))
        return res

    def fw_arrivals(i):
        res = []
        for j, q in enumerate((gs, (gs + 2) % 4)):
            _, d = wx_pieces(zp, q, z)[i]
            res.append(remote(d, d, fws.at[i, j], fwr.at[i, j], (gs, t)))
        return res

    for i in range(4):
        for c in wx_copies(i):
            c.start()
    for i in (1, 2, 5, 6, 3, 7):
        local[i].start()

    metap[...] = dot(perm, meta[...])
    idx = metap[:, :128]
    lane = lax.broadcasted_iota(jnp.int32, (TOKENS, 128), 1)
    idxi = idx.astype(jnp.int32)

    local[4].wait()
    acc[:, :128] = jnp.zeros((TOKENS, 128), F32)

    def low_step(a, carry):
        part = dot(hb[0, 0], dn[a])
        acc[:, :128] = acc[:, :128] + jnp.where(idxi == a, part, 0.0)
        return carry

    lax.fori_loop(0, ADAPTERS, low_step, 0)
    lowsend[...] = acc[:, :128].astype(BF16).reshape(32, 16, 128)

    def low_copy(o):
        d = (t + o) % 32
        return remote(lowsend.at[d], lowrecv.at[t], lows, lowr, (g, d))

    def low_start(o, carry):
        low_copy(o).start()
        return carry

    lax.fori_loop(1, 32, low_start, 0)
    lowrecv[t] = lowsend[t]

    def arrive(row, kind):
        ag[row][kind].wait_recv()

    arrive(0, 0)
    ag[0][2].start()
    ag[2][0].start()
    ag[2][1].start()
    arrive(0, 1)
    ag[0][3].start()
    ag[4][0].start()
    ag[4][1].start()
    arrive(1, 0)
    ag[1][2].start()
    arrive(1, 1)
    ag[1][3].start()

    remote(lowrecv.at[pl.ds(0, 31)], lowrecv.at[pl.ds(0, 31)], lows, lowr, (g, tp)).wait_recv()
    lowrank = jnp.sum(lowrecv[...].astype(F32), axis=0)
    bucket = metap[pl.ds(pl.multiple_of(t * 16, 16), 16), 128:]
    lane16 = lax.broadcasted_iota(jnp.int32, (16, 128), 1) % RANK_LIMIT
    scaled = jnp.where(lane16.astype(F32) < bucket, lowrank * (0.5 * RANK_LIMIT) / bucket, 0.0)
    scown[...] = scaled.astype(BF16)

    def sc_copy(o):
        d = (t + o) % 32
        return remote(scown, screcv.at[t], scs, scr, (g, d))

    def sc_start(o, carry):
        sc_copy(o).start()
        return carry

    lax.fori_loop(1, 32, sc_start, 0)
    screcv[t] = scown[...]

    arrive(0, 2)
    arrive(0, 3)
    ag[3][0].start()
    ag[3][1].start()

    for i in (0, 1, 2):
        local[i].wait()
        for a, c in zip(wx_arrivals(i), fw_copies(i)):
            a.wait_recv()
            c.start()
    for i in (0, 1, 2):
        for a in fw_arrivals(i):
            a.wait_recv()

    acc[...] = jnp.zeros(acc.shape, F32)

    def project(oa, ob):
        k0 = pl.multiple_of(slice_index(oa, ob) * 256, 256)
        h = hb[oa, ob]
        acc[:, 0:256] = acc[:, 0:256] + dot(h, wq[pl.ds(k0, 256)])
        acc[:, 256:512] = acc[:, 256:512] + dot(h, wqp[pl.ds(k0, 256)])
        acc[:, 512:640] = acc[:, 512:640] + dot_nt(h, kvt[:, pl.ds(k0, 256)])

    for o in range(4):
        project(o, 0)
    project(0, 1)
    project(0, 3)

    for oa in (1, 3):
        arrive(1 + oa, 0)
        ag[1 + oa][2].start()
        arrive(1 + oa, 1)
        ag[1 + oa][3].start()
        project(oa, 1)
        project(oa, 3)

    remote(screcv.at[pl.ds(0, 31)], screcv.at[pl.ds(0, 31)], scs, scr, (g, tp)).wait_recv()
    local[5].wait()
    local[6].wait()
    sc = screcv[...].reshape(TOKENS, 128).astype(F32)
    swapped = pltpu.roll(sc, 64, 1)
    sq = jnp.where(lane < 64, sc, swapped).astype(BF16)
    sv = jnp.where(lane < 64, swapped, 0.0).astype(BF16)
    lift[...] = jnp.zeros(lift.shape, F32)

    def lift_step(j, carry):
        mine = jnp.where(idxi == 2 * j + lane // 64, sq.astype(F32), 0.0).astype(BF16)
        lift[...] = lift[...] + dot(mine, uq[pl.ds(pl.multiple_of(j * 128, 128), 128)])
        return carry

    lax.fori_loop(0, ADAPTERS // 2, lift_step, 0)
    liftv[...] = jnp.zeros(liftv.shape, F32)
    svk = sv[:, :64]

    def liftv_step(j, carry):
        part = dot_nt(svk, uv[pl.ds(pl.multiple_of(j * 128, 128), 128)])
        liftv[...] = liftv[...] + jnp.where(idxi == 4 * j + lane // 32, part, 0.0)
        return carry

    lax.fori_loop(0, ADAPTERS // 4, liftv_step, 0)
    lv = liftv[...]
    lv = lv + pltpu.roll(lv, 64, 1)
    lv = lv + pltpu.roll(lv, 32, 1)
    place = lane // 32 == 2 * z + 1
    liftv[...] = jnp.where(place, lv, 0.0)

    arrive(3, 0)
    ag[3][2].start()
    arrive(3, 1)
    ag[3][3].start()
    project(2, 1)
    project(2, 3)
    for oa in (0, 1, 3, 2):
        arrive(1 + oa, 2)
        arrive(1 + oa, 3)
        project(oa, 2)

    def message(v, block):
        m = v.astype(F32).reshape(32, 2, 8, 128)
        for l in range(2):
            send1[l, :, block] = m[:, l].astype(BF16)

    for j in range(2):
        cols = pl.ds(j * 128, 128)
        message(acc[:, j * 128:(j + 1) * 128] + lift[:, j * 128:(j + 1) * 128], 2 * z + j)
        message(acc[:, 256 + j * 128:256 + (j + 1) * 128], 2 * zp + j)
    message(acc[:, 512:640] + liftv[...], 4)

    def s1_copy(l, o):
        d = (t + o) % 32
        return remote(send1.at[l, d], recv1.at[l, t], s1s.at[l], s1r.at[l], ((g + l) % 4, d))

    def s1_start(o, carry):
        s1_copy(1, o).start()
        s1_copy(0, o).start()
        return carry

    lax.fori_loop(1, 32, s1_start, 0)
    s1_copy(1, 0).start()
    recv1[0, t] = send1[0, t]

    local[3].wait()
    for a, c in zip(wx_arrivals(3), fw_copies(3)):
        a.wait_recv()
        c.start()

    local[7].wait()
    remote(recv1.at[0, pl.ds(0, 31)], recv1.at[0, pl.ds(0, 31)], s1s.at[0], s1r.at[0], (g, tp)).wait_recv()
    remote(recv1.at[1], recv1.at[1], s1s.at[1], s1r.at[1], (g, tp)).wait_recv()

    for l in range(2):
        cos8 = cos_t[l * 8:(l + 1) * 8, :][None]
        sin8 = sin_t[l * 8:(l + 1) * 8, :][None]
        for yx in range(16):
            m = recv1[l, yx].astype(F32) + recv1[l, 16 + yx].astype(F32)
            m = m.astype(BF16).astype(F32)
            q = m[:4]
            q = q * cos8 + pltpu.roll(q, 64, 2) * sin8
            for zj in range(4):
                head = (zj // 2) * 32 + yx * 2 + zj % 2
                r0 = l * 512 + head * 8
                qs[r0:r0 + 8, :] = q[zj].astype(BF16).astype(F32)
            yy, xx = yx // 4, yx % 4
            r0 = (l * 4 + yy) * 8
            kvs[r0:r0 + 8, xx * 128:(xx + 1) * 128] = m[4]

    i0 = lax.broadcasted_iota(jnp.int32, (512, 512), 0)
    i1 = lax.broadcasted_iota(jnp.int32, (512, 512), 1)
    target = ((i0 // 32) % 2) * 256 + ((i0 // 64) % 2) * 128 + (i0 // 128) * 32 + i0 % 32
    kvp = dot(kvs[...].astype(BF16), (target == i1).astype(BF16))
    for l in range(2):
        cos8 = cos_t[l * 8:(l + 1) * 8, :]
        sin8 = sin_t[l * 8:(l + 1) * 8, :]
        for yy in range(4):
            r0 = (l * 4 + yy) * 8
            for zz in range(2):
                k = kvp[r0:r0 + 8, zz * 128:(zz + 1) * 128]
                k = k * cos8 + pltpu.roll(k, 64, 1) * sin8
                n = zz * 4 + yy
                knf[l * 8:(l + 1) * 8, n * 128:(n + 1) * 128] = k
                vnf[l * 8:(l + 1) * 8, n * 128:(n + 1) * 128] = kvp[r0:r0 + 8, 256 + zz * 128:256 + (zz + 1) * 128]
    knew = knf[...].astype(BF16)
    vnew = vnf[...].astype(BF16)

    head_of = lax.broadcasted_iota(jnp.int32, (128, 128), 0) % 64
    pos = lax.broadcasted_iota(jnp.int32, (272, 128), 0)
    step = lax.broadcasted_iota(jnp.int32, (272, 128), 1) // 64

    def attend(i, carry):
        l = i // 4
        ii = i % 4
        base = l * 512 + 2 * ii
        q = jnp.concatenate([qs[pl.ds(base + s, 64, stride=8), :] for s in range(2)], axis=0)
        bd = jnp.concatenate(
            [jnp.where(head_of // 8 == n, q, 0.0).astype(BF16) for n in range(8)], axis=1
        )
        keys = jnp.concatenate([pages[pids[i, j], :, :1024] for j in range(4)] + [knew], axis=0)
        values = jnp.concatenate([pages[pids[i, j], :, 1024:] for j in range(4)] + [vnew], axis=0)
        scores = dot_nt(keys, bd) * HEAD_SIZE ** (-0.5)
        first = 256 + 2 * i
        usable = (pos < lens[i]) | (pos == first) | ((pos == first + 1) & (step == 1))
        top = jnp.max(jnp.where(usable, scores, -jnp.inf), axis=0, keepdims=True)
        e = jnp.where(usable, jnp.exp(scores - top), 0.0)
        p = (e / jnp.sum(e, axis=0, keepdims=True)).astype(BF16)
        o = dot_tn(p, values)
        for s in range(2):
            for n in range(8):
                att[pl.ds(pl.multiple_of((2 * i + s) * 64 + n * 8, 8), 8), :] = o[
                    s * 64 + n * 8:s * 64 + (n + 1) * 8, n * 128:(n + 1) * 128
                ]
        return carry

    lax.fori_loop(0, 8, attend, 0)

    def pack2(yx, carry):
        for l in range(2):
            for zj in range(4):
                head = (zj // 2) * 32 + yx * 2 + zj % 2
                send2[l, yx, zj] = att[pl.ds(l * 512 + head, 8, stride=64), :].astype(BF16)
        return carry

    lax.fori_loop(0, 16, pack2, 0)

    def s2_copy(l, o):
        d = (t + o) % 32
        return remote(send2.at[l, d % 16], recv2.at[l, t], s2s.at[l], s2r.at[l], ((g + 4 - l) % 4, d))

    def s2_start(o, carry):
        s2_copy(1, o).start()
        s2_copy(0, o).start()
        return carry

    lax.fori_loop(1, 32, s2_start, 0)
    s2_copy(1, 0).start()
    recv2[0, t] = send2[0, t % 16]

    for a in fw_arrivals(3):
        a.wait_recv()
    remote(recv2.at[0, pl.ds(0, 31)], recv2.at[0, pl.ds(0, 31)], s2s.at[0], s2r.at[0], (g, tp)).wait_recv()
    remote(recv2.at[1], recv2.at[1], s2s.at[1], s2r.at[1], (g, tp)).wait_recv()

    def build(s, carry):
        r0 = pl.multiple_of(s * 16, 16)
        for zj in range(4):
            both = jnp.concatenate([recv2[l, s, zj].astype(F32) for l in range(2)], axis=0)
            lhs[pl.ds(r0, 16), zj * 128:(zj + 1) * 128] = both.astype(BF16)
        return carry

    lax.fori_loop(0, 32, build, 0)

    def partial(oa, ob):
        c0 = pl.multiple_of(slice_index(oa, ob) * 256, 256)
        return dot(lhs[:, :256], wo[0, :, pl.ds(c0, 256)]) + dot(lhs[:, 256:], wo[1, :, pl.ds(c0, 256)])

    def rs_copy(row, kind):
        along_b = 1 if row else 0
        oa = row - 1

        def src(o, rows=None):
            ref = sb.at[oa, o] if along_b else ta.at[o]
            return ref if rows is None else ref.at[pl.ds(rows, 256)]

        halves = rh.at[oa] if along_b else rah
        fulls = rf.at[oa] if along_b else raf
        if kind == 0:
            s, d, way = src(2, 0), halves.at[0], -1
        elif kind == 1:
            s, d, way = src(2, 256), halves.at[1], 1
        elif kind == 2:
            s, d, way = src(3), fulls.at[0], -1
        else:
            s, d, way = src(1), fulls.at[1], 1
        return remote(s, d, rss.at[row, kind], rsr.at[row, kind], near(along_b, way))

    rs = [[rs_copy(row, kind) for kind in range(4)] for row in range(5)]
    order = (2, 1, 3, 0)
    for oa in order:
        sb[oa, 2] = partial(oa, 2).astype(BF16)
        rs[1 + oa][0].start()
        rs[1 + oa][1].start()
    for oa in order:
        sf[oa, 2] = partial(oa, 3)
        rs[1 + oa][0].wait_recv()
        sb[oa, 3, 0:256] = (sf[oa, 2, 0:256] + rh[oa, 0].astype(F32)).astype(BF16)
        sb[oa, 3, 256:512] = sf[oa, 2, 256:512].astype(BF16)
        rs[1 + oa][2].start()
        sf[oa, 1] = partial(oa, 1)
        rs[1 + oa][1].wait_recv()
        sb[oa, 1, 0:256] = sf[oa, 1, 0:256].astype(BF16)
        sb[oa, 1, 256:512] = (sf[oa, 1, 256:512] + rh[oa, 1].astype(F32)).astype(BF16)
        rs[1 + oa][3].start()
    for oa in order:
        sf[oa, 0] = partial(oa, 0)

    def total(oa):
        rs[1 + oa][2].wait_recv()
        rs[1 + oa][3].wait_recv()
        return sf[oa, 0] + rf[oa, 0].astype(F32) + rf[oa, 1].astype(F32)

    ta[2] = total(2).astype(BF16)
    rs[0][0].start()
    rs[0][1].start()
    sf[1, 0] = total(1)
    rs[0][1].wait_recv()
    ta[1, 0:256] = sf[1, 0, 0:256].astype(BF16)
    ta[1, 256:512] = (sf[1, 0, 256:512] + rah[1].astype(F32)).astype(BF16)
    rs[0][3].start()
    sf[3, 0] = total(3)
    rs[0][0].wait_recv()
    ta[3, 0:256] = (sf[3, 0, 0:256] + rah[0].astype(F32)).astype(BF16)
    ta[3, 256:512] = sf[3, 0, 256:512].astype(BF16)
    rs[0][2].start()
    sf[0, 0] = total(0)
    rs[0][2].wait_recv()
    rs[0][3].wait_recv()
    final = (sf[0, 0] + raf[0].astype(F32) + raf[1].astype(F32)).astype(BF16)
    back = (lax.broadcasted_iota(jnp.int32, (TOKENS, TOKENS), 1) == pos_col[...]).astype(BF16)
    out[...] = dot(back, final).astype(BF16)

    for row in range(5):
        for kind in range(4):
            ag[row][kind].wait_send()
            rs[row][kind].wait_send()
    for i in range(4):
        for c in wx_copies(i) + fw_copies(i):
            c.wait_send()
    remote(lowrecv.at[pl.ds(0, 31)], lowrecv.at[pl.ds(0, 31)], lows, lowr, (g, tp)).wait_send()
    remote(screcv.at[pl.ds(0, 31)], screcv.at[pl.ds(0, 31)], scs, scr, (g, tp)).wait_send()
    remote(recv1.at[0, pl.ds(0, 31)], recv1.at[0, pl.ds(0, 31)], s1s.at[0], s1r.at[0], (g, tp)).wait_send()
    remote(recv1.at[1], recv1.at[1], s1s.at[1], s1r.at[1], (g, tp)).wait_send()
    remote(recv2.at[0, pl.ds(0, 31)], recv2.at[0, pl.ds(0, 31)], s2s.at[0], s2r.at[0], (g, tp)).wait_send()
    remote(recv2.at[1], recv2.at[1], s2s.at[1], s2r.at[1], (g, tp)).wait_send()


def scratch():
    v = pltpu.VMEM
    dma = pltpu.SemaphoreType.DMA
    return [
        v((4, 4, 512, 256), BF16),
        v((4096, 256), BF16),
        v((4096, 256), BF16),
        v((128, 4096), BF16),
        v((2, 256, 4096), BF16),
        v((32, 64, 2048), BF16),
        v((32, 256, 128), BF16),
        v((2048, 256), BF16),
        v((1024, 64), BF16),
        v((512, 640), F32),
        v((512, 256), F32),
        v((32, 16, 128), BF16),
        v((32, 16, 128), BF16),
        v((16, 128), BF16),
        v((32, 16, 128), BF16),
        v((512, 256), F32),
        v((512, 128), F32),
        v((2, 32, 5, 8, 128), BF16),
        v((2, 32, 5, 8, 128), BF16),
        v((1024, 128), F32),
        v((64, 512), F32),
        v((16, 1024), F32),
        v((16, 1024), F32),
        v((1024, 128), F32),
        v((2, 16, 4, 8, 128), BF16),
        v((2, 32, 4, 8, 128), BF16),
        v((512, 512), BF16),
        v((4, 4, 512, 256), BF16),
        v((4, 3, 512, 256), F32),
        v((4, 2, 256, 256), BF16),
        v((4, 2, 512, 256), BF16),
        v((4, 512, 256), BF16),
        v((2, 256, 256), BF16),
        v((2, 512, 256), BF16),
        dma((8,)),
        dma((5, 4)), dma((5, 4)),
        dma((4, 2)), dma((4, 2)),
        dma((4, 2)), dma((4, 2)),
        dma, dma, dma, dma,
        dma((2,)), dma((2,)),
        dma((2,)), dma((2,)),
        dma((5, 4)), dma((5, 4)),
    ]


def local(
    hidden, query_weight, key_weight, value_weight, output_weight, adapter_down_maps,
    adapter_up_query, adapter_up_value, key_value_pages, row_adapter_index,
    row_rank_bucket, lengths, row_page_index,
):
    g = lax.axis_index("group")
    t = lax.axis_index("tensor")
    i32 = jnp.int32

    table = lax.dynamic_slice_in_dim(row_page_index, g * 256, 256, 0)
    block = jnp.arange(256, dtype=i32) // ROWS_DEV
    flags = (table[:, 0] // POOL != g * 32 + block).astype(i32).reshape(32, 8)
    earlier = (jnp.arange(8)[:, None] > jnp.arange(8)[None, :]).astype(i32)

    def places(f):
        before = jnp.sum(earlier * f[..., None, :], axis=-1)
        return jnp.where(f == 1, RES + before, jnp.arange(8, dtype=i32) - before)

    place = places(flags).reshape(256)
    pos = (block * 16 + place * 2)[:, None] + jnp.arange(STEPS, dtype=i32)[None, :]
    pos = pos.reshape(TOKENS)

    base = (g * 32 + t) * POOL
    lens, pids = [], []
    for l in range(2):
        gg = (g + 4 - l) % 4
        first = gg * 256 + t * ROWS_DEV
        tab = lax.dynamic_slice_in_dim(row_page_index, first, ROWS_DEV, 0)
        lng = lax.dynamic_slice_in_dim(lengths, first, ROWS_DEV, 0)
        pl8 = places((tab[:, 0] // POOL != gg * 32 + t).astype(i32))
        sel = (pl8[None, :] == l * RES + jnp.arange(4, dtype=i32)[:, None]).astype(i32)
        lens.append(jnp.sum(sel * lng[None, :], axis=1))
        pids.append(jnp.sum(sel[:, :, None] * tab[None], axis=1))
    lens = jnp.concatenate(lens)
    pids = jnp.clip(jnp.concatenate(pids) - base, 0, POOL - 1)
    positions = (lens[:, None] + jnp.arange(STEPS, dtype=i32)[None, :]).reshape(16)
    inverse_freq = jnp.exp(-math.log(ROPE_BASE) * jnp.arange(64, dtype=F32) / 64)
    angles = positions.astype(F32)[:, None] * jnp.concatenate([inverse_freq, inverse_freq])[None]
    cos_t = jnp.cos(angles)
    sin_t = jnp.sin(angles) * jnp.where(jnp.arange(128) < 64, -1.0, 1.0)[None]

    meta = jnp.stack([row_adapter_index, row_rank_bucket], axis=1).astype(BF16)
    meta = jnp.broadcast_to(meta[:, None, :, None], (256, STEPS, 2, 128)).reshape(TOKENS, 256)

    vm = pl.BlockSpec(memory_space=pltpu.VMEM)
    sm = pl.BlockSpec(memory_space=pltpu.SMEM)
    hbm = pl.BlockSpec(memory_space=pl.ANY)
    res = pl.pallas_call(
        kernel,
        out_shape=jax.ShapeDtypeStruct((TOKENS, 256), BF16),
        in_specs=[vm] * 6 + [sm] * 2 + [hbm] * 8,
        out_specs=vm,
        scratch_shapes=scratch(),
        compiler_params=pltpu.CompilerParams(
            has_side_effects=True, vmem_limit_bytes=60 * 1024 * 1024
        ),
    )(
        hidden.reshape(TOKENS, 256), meta, pos[None, :], pos[:, None], cos_t, sin_t, lens, pids,
        query_weight, key_weight.T, value_weight.T, output_weight, adapter_down_maps,
        adapter_up_query.reshape(2048, 256),
        adapter_up_value.transpose(0, 2, 1).reshape(1024, 64), key_value_pages,
    )
    return res.reshape(256, STEPS, 256)


def solution(mesh):
    in_specs = (
        P("group", None, "tensor"),
        P(None, "tensor"),
        P(None, "tensor"),
        P(None, "tensor"),
        P("tensor", None),
        P(None, "tensor", None),
        P(None, None, "tensor"),
        P(None, None, "tensor"),
        P(("group", "tensor"), None, None),
        P("group"),
        P("group"),
        P(),
        P(),
    )
    out_specs = P("group", None, "tensor")
    return jax.shard_map(local, mesh=mesh, in_specs=in_specs, out_specs=out_specs, check_vma=False)
```

```python
import functools
import math

import jax
import jax.numpy as jnp
import numpy as np
from jax import lax
from jax.experimental import pallas as pl
from jax.experimental.pallas import tpu as pltpu
from jax.sharding import PartitionSpec as P

QUERY_HEADS = 64
KEY_VALUE_HEADS = 8
HEAD_SIZE = 128
RANK_LIMIT = 64
ADAPTERS = 32
STEPS = 2
RES = 4
ROWS_DEV = 8
TOKENS = 512
POOL = 32
ROPE_BASE = 500000.0
MESH = pl.DeviceIdType.MESH
F32 = jnp.float32
BF16 = jnp.bfloat16


def dot(a, b):
    return jnp.dot(a, b, preferred_element_type=F32)


def dot_nt(a, b):
    return lax.dot_general(a, b, (((1,), (1,)), ((), ())), preferred_element_type=F32)


def dot_tn(a, b):
    return lax.dot_general(a, b, (((0,), (0,)), ((), ())), preferred_element_type=F32)


def remote(src, dst, send, recv, device):
    return pltpu.make_async_remote_copy(
        src_ref=src, dst_ref=dst, send_sem=send, recv_sem=recv,
        device_id=device, device_id_type=MESH,
    )


def kernel(
    hid, adapters, buckets, table_v, cos_tab, sin_tab, lengths, table,
    qw, kt, vt, ow, down, upq, upv, pool,
    out,
    hb, wq, wqp, kvt, wo, pages, dn, uq, uv,
    cos_t, sin_t, lens, pids, back,
    acc, metap, lowsend, lowrecv, scown, screcv, lift, liftv,
    send1, recv1, qs, kvs, knf, vnf, att, send2, recv2, lhs,
    sb, sf, rh, rf, ta, rah, raf,
    loc, ags, agr, wxs, wxr, fws, fwr, lows, lowr, scs, scr, s1s, s1r, s2s, s2r, rss, rsr, plane_sem, all_sem,
):
    g = lax.axis_index("group")
    t = lax.axis_index("tensor")
    core = g % 2
    z = t // 16
    y = (t // 4) % 4
    x = t % 4
    zp = 1 - z
    tp = zp * 16 + y * 4 + x
    g2 = (g + 2) % 4
    gs = g + 1 - 2 * core

    def near(along_b, d):
        on_x = (1 - core) * (1 - along_b) + core * along_b
        on_y = 1 - on_x
        xx = (x + 4 + d * on_x) % 4
        yy = (y + 4 + d * on_y) % 4
        return (g, z * 16 + yy * 4 + xx)

    def slice_index(oa, ob):
        dx = oa * (1 - core) + ob * core
        dy = oa * core + ob * (1 - core)
        return ((y + dy) % 4) * 4 + (x + dx) % 4

    half = z * 4096
    local = [
        (qw.at[pl.ds(pl.multiple_of(half, 4096), 4096)], wq),
        (kt.at[:, pl.ds(pl.multiple_of(half, 4096), 4096)], kvt.at[pl.ds(pl.multiple_of(z * 64, 32), 32)]),
        (vt.at[:, pl.ds(pl.multiple_of(half, 4096), 4096)], kvt.at[pl.ds(pl.multiple_of(z * 64 + 32, 32), 32)]),
        (ow.at[:, pl.ds(pl.multiple_of(half, 4096), 4096)], wo.at[z]),
        (down, dn),
        (upq, uq),
        (upv, uv),
        (pool, pages),
    ]
    local = [pltpu.make_async_copy(s, d, loc.at[i]) for i, (s, d) in enumerate(local)]
    local[4].start()
    local[0].start()

    barrier = pltpu.get_barrier_semaphore()

    def ring_x(d):
        return (g, z * 16 + y * 4 + (x + d) % 4)

    def ring_y(d):
        return (g, z * 16 + ((y + d) % 4) * 4 + x)

    def line_z(d):
        zz = (2 * (g // 2) + z + d // 2) % 4
        return ((zz // 2) * 2 + (core + d) % 2, (zz % 2) * 16 + y * 4 + x)

    def greet(sem, device):
        pl.semaphore_signal(sem, inc=1, device_id=device, device_id_type=MESH)

    for d in range(1, 4):
        greet(barrier, ring_x(d))
        greet(barrier, ring_y(d))
    for d in range(1, 8):
        greet(barrier, line_z(d))

    def iota(shape, dim):
        return lax.broadcasted_iota(jnp.int32, shape, dim)

    tok = iota((8, TOKENS), 1)
    spread = (iota((256, TOKENS), 0) == iota((256, TOKENS), 1) // 2).astype(BF16)
    ahead = (
        (iota((256, TOKENS), 0) // 8 == iota((256, TOKENS), 1) // 16)
        & (iota((256, TOKENS), 0) < iota((256, TOKENS), 1) // 2)
    ).astype(BF16)
    first_page = table_v[0:1, pl.ds(pl.multiple_of(g * 256, 256), 256)]
    moved = (first_page // POOL != g * 32 + iota((1, 256), 1) // 8).astype(F32)
    moved = jnp.broadcast_to(moved, (8, 256)).astype(BF16)
    resumed = dot(moved, spread).astype(jnp.int32)
    before = dot(moved, ahead).astype(jnp.int32)
    place = jnp.where(resumed == 1, before, (tok // 2) % 8 - before)
    pos = resumed * 256 + (tok // 16) * 8 + place * 2 + tok % 2
    perm = (iota((TOKENS, TOKENS), 0) == pos[0:1]).astype(BF16)
    hb[0, 0] = dot(perm, hid[...]).astype(BF16)

    def ag_copy(row, kind):
        along_b = 1 if row else 0
        oa = row - 1

        def at(o, rows=None):
            ref = hb.at[oa, o] if along_b else hb.at[o, 0]
            return ref if rows is None else ref.at[pl.ds(rows, 256)]

        if kind == 0:
            src, dst, d = at(0), at(1), -1
        elif kind == 1:
            src, dst, d = at(0), at(3), 1
        elif kind == 2:
            src, dst, d = at(1, 0), at(2, 0), -1
        else:
            src, dst, d = at(3, 256), at(2, 256), 1
        return remote(src, dst, ags.at[row, kind], agr.at[row, kind], near(along_b, d))

    ag = [[ag_copy(row, kind) for kind in range(4)] for row in range(5)]
    pl.semaphore_wait(barrier, 13)
    for row in (0, 1):
        for kind in (0, 1):
            ag[row][kind].start()
    for d in range(1, 4):
        greet(plane_sem, ring_y(d))

    def wx_pieces(zq, q, zd):
        c0 = pl.multiple_of(zd * 4096 + q * 1024, 1024)
        d0 = pl.multiple_of(q * 1024, 1024)
        r0 = pl.multiple_of(q * 64, 64)
        return [
            (qw.at[pl.ds(c0, 1024)], wqp.at[pl.ds(d0, 1024)]),
            (kt.at[:, pl.ds(c0, 1024)], kvt.at[pl.ds(pl.multiple_of(zq * 64, 32), 32), pl.ds(d0, 1024)]),
            (vt.at[:, pl.ds(c0, 1024)], kvt.at[pl.ds(pl.multiple_of(zq * 64 + 32, 32), 32), pl.ds(d0, 1024)]),
            (ow.at[pl.ds(r0, 64), pl.ds(pl.multiple_of(zd * 4096, 4096), 4096)], wo.at[zq, pl.ds(r0, 64)]),
        ]

    def wx_copies(i):
        s, d = wx_pieces(z, g, zp)[i]
        return [remote(s, d, wxs.at[i, j], wxr.at[i, j], (gd, tp)) for j, gd in enumerate((g, g2))]

    def wx_arrivals(i):
        res = []
        for j, q in enumerate((g, g2)):
            s, d = wx_pieces(zp, q, z)[i]
            res.append(remote(s, d, wxs.at[i, j], wxr.at[i, j], (g, tp)))
        return res

    def fw_copies(i):
        res = []
        for j, q in enumerate((g, g2)):
            _, d = wx_pieces(zp, q, z)[i]
            res.append(remote(d, d, fws.at[i, j], fwr.at[i, j], (gs, t)))
        return res

    def fw_arrivals(i):
        res = []
        for j, q in enumerate((gs, (gs + 2) % 4)):
            _, d = wx_pieces(zp, q, z)[i]
            res.append(remote(d, d, fws.at[i, j], fwr.at[i, j], (gs, t)))
        return res

    for i in range(4):
        for c in wx_copies(i):
            c.start()
    for i in (1, 2, 5, 6, 3, 7):
        local[i].start()

    def along(row):
        wide = jnp.broadcast_to(row.astype(F32), (128, 256)).astype(BF16)
        return dot_nt(perm, dot(wide, spread).astype(BF16))

    metap[:, :128] = along(adapters[...])
    metap[:, 128:] = along(buckets[...])
    pl.semaphore_wait(plane_sem, 3)
    for d in range(1, 8):
        greet(all_sem, line_z(d))
    eye = (iota((TOKENS, TOKENS), 0) == iota((TOKENS, TOKENS), 1)).astype(BF16)
    back[...] = dot_nt(eye, perm).astype(BF16)

    base = (g * 32 + t) * POOL
    for l in range(2):
        gg = (g + 4 - l) % 4
        first = gg * 256 + t * ROWS_DEV
        marks, spots = [], []
        count = jnp.int32(0)
        for k in range(ROWS_DEV):
            mark = jnp.where(table[0, first + k] // POOL != gg * 32 + t, 1, 0)
            marks.append(mark)
            spots.append(jnp.where(mark == 1, count, k - count))
            count = count + mark
        for i in range(RES):
            mine = [(marks[k] == l) & (spots[k] == i) for k in range(ROWS_DEV)]
            row = l * RES + i
            lens[row] = sum(jnp.where(mine[k], lengths[first + k], 0) for k in range(ROWS_DEV))
            for j in range(4):
                page = sum(jnp.where(mine[k], table[j, first + k], 0) for k in range(ROWS_DEV))
                pids[row, j] = jnp.clip(page - base, 0, POOL - 1)
            cos_t[2 * row:2 * row + 2, :] = cos_tab[pl.ds(lens[row], 2), :]
            sin_t[2 * row:2 * row + 2, :] = sin_tab[pl.ds(lens[row], 2), :]
    idx = metap[:, :128]
    lane = lax.broadcasted_iota(jnp.int32, (TOKENS, 128), 1)
    idxi = idx.astype(jnp.int32)

    local[4].wait()
    acc[:, :128] = jnp.zeros((TOKENS, 128), F32)

    def low_step(a, carry):
        part = dot(hb[0, 0], dn[a])
        acc[:, :128] = acc[:, :128] + jnp.where(idxi == a, part, 0.0)
        return carry

    lax.fori_loop(0, ADAPTERS, low_step, 0)
    for l in range(2):
        lowsend[:, l] = acc[l * 256:(l + 1) * 256, :128].reshape(32, 8, 128).astype(BF16)
    pl.semaphore_wait(all_sem, 7)

    def low_copy(o):
        d = (t + o) % 32
        return remote(lowsend.at[d], lowrecv.at[t], lows, lowr, (g, d))

    def low_start(o, carry):
        low_copy(o).start()
        return carry

    lax.fori_loop(1, 32, low_start, 0)
    lowrecv[t] = lowsend[t]

    def arrive(row, kind):
        ag[row][kind].wait_recv()

    arrive(0, 0)
    ag[0][2].start()
    ag[2][0].start()
    ag[2][1].start()
    arrive(0, 1)
    ag[0][3].start()
    ag[4][0].start()
    ag[4][1].start()
    arrive(1, 0)
    ag[1][2].start()
    arrive(1, 1)
    ag[1][3].start()

    remote(lowrecv.at[pl.ds(0, 31)], lowrecv.at[pl.ds(0, 31)], lows, lowr, (g, tp)).wait_recv()
    lane16 = lax.broadcasted_iota(jnp.int32, (8, 128), 1) % RANK_LIMIT
    for l in range(2):
        lowrank = jnp.sum(lowrecv[:, l].astype(F32), axis=0)
        bucket = metap[pl.ds(pl.multiple_of(l * 256 + t * 8, 8), 8), 128:]
        scaled = jnp.where(lane16.astype(F32) < bucket, lowrank * (0.5 * RANK_LIMIT) / bucket, 0.0)
        scown[l] = scaled.astype(BF16)

    def sc_copy(o):
        d = (t + o) % 32
        return remote(scown, screcv.at[t], scs, scr, (g, d))

    def sc_start(o, carry):
        sc_copy(o).start()
        return carry

    lax.fori_loop(1, 32, sc_start, 0)
    screcv[t] = scown[...]

    arrive(0, 2)
    arrive(0, 3)
    ag[3][0].start()
    ag[3][1].start()

    for i in (0, 1, 2):
        local[i].wait()
        for a, c in zip(wx_arrivals(i), fw_copies(i)):
            a.wait_recv()
            c.start()
    for i in (0, 1, 2):
        for a in fw_arrivals(i):
            a.wait_recv()

    acc[...] = jnp.zeros(acc.shape, F32)

    def project(oa, ob):
        k0 = pl.multiple_of(slice_index(oa, ob) * 256, 256)
        h = hb[oa, ob]
        acc[:, 0:256] = acc[:, 0:256] + dot(h, wq[pl.ds(k0, 256)])
        acc[:, 256:512] = acc[:, 256:512] + dot(h, wqp[pl.ds(k0, 256)])
        acc[:, 512:640] = acc[:, 512:640] + dot_nt(h, kvt[:, pl.ds(k0, 256)])

    for o in range(4):
        project(o, 0)
    project(0, 1)
    project(0, 3)

    for oa in (1, 3):
        arrive(1 + oa, 0)
        ag[1 + oa][2].start()
        arrive(1 + oa, 1)
        ag[1 + oa][3].start()
        project(oa, 1)
        project(oa, 3)

    remote(screcv.at[pl.ds(0, 31)], screcv.at[pl.ds(0, 31)], scs, scr, (g, tp)).wait_recv()
    local[5].wait()
    local[6].wait()
    sc = jnp.concatenate([screcv[:, l].astype(F32).reshape(256, 128) for l in range(2)], axis=0)
    swapped = pltpu.roll(sc, 64, 1)
    sq = jnp.where(lane < 64, sc, swapped).astype(BF16)
    sv = jnp.where(lane < 64, swapped, 0.0).astype(BF16)
    lift[...] = jnp.zeros(lift.shape, F32)

    def lift_step(j, carry):
        mine = jnp.where(idxi == 2 * j + lane // 64, sq.astype(F32), 0.0).astype(BF16)
        lift[...] = lift[...] + dot(mine, uq[pl.ds(pl.multiple_of(j * 128, 128), 128)])
        return carry

    lax.fori_loop(0, ADAPTERS // 2, lift_step, 0)
    liftv[...] = jnp.zeros(liftv.shape, F32)
    svk = sv[:, :64]

    def liftv_step(j, carry):
        part = dot_nt(svk, uv[pl.ds(pl.multiple_of(j * 128, 128), 128)])
        liftv[...] = liftv[...] + jnp.where(idxi == 4 * j + lane // 32, part, 0.0)
        return carry

    lax.fori_loop(0, ADAPTERS // 4, liftv_step, 0)
    lv = liftv[...]
    lv = lv + pltpu.roll(lv, 64, 1)
    lv = lv + pltpu.roll(lv, 32, 1)
    place = lane // 32 == 2 * z + 1
    liftv[...] = jnp.where(place, lv, 0.0)

    arrive(3, 0)
    ag[3][2].start()
    arrive(3, 1)
    ag[3][3].start()
    project(2, 1)
    project(2, 3)
    for oa in (0, 1, 3, 2):
        arrive(1 + oa, 2)
        arrive(1 + oa, 3)
        project(oa, 2)

    def message(v, block):
        m = v.reshape(2, 32, 8, 128)
        for l in range(2):
            send1[l, :, block] = m[l].astype(BF16)

    for j in range(2):
        cols = pl.ds(j * 128, 128)
        message(acc[:, j * 128:(j + 1) * 128] + lift[:, j * 128:(j + 1) * 128], 2 * z + j)
        message(acc[:, 256 + j * 128:256 + (j + 1) * 128], 2 * zp + j)
    message(acc[:, 512:640] + liftv[...], 4)

    def s1_copy(l, o):
        d = (t + o) % 32
        return remote(send1.at[l, d], recv1.at[l, t], s1s.at[l], s1r.at[l], ((g + l) % 4, d))

    def s1_start(o, carry):
        s1_copy(1, o).start()
        s1_copy(0, o).start()
        return carry

    lax.fori_loop(1, 32, s1_start, 0)
    s1_copy(1, 0).start()
    recv1[0, t] = send1[0, t]

    local[3].wait()
    for a, c in zip(wx_arrivals(3), fw_copies(3)):
        a.wait_recv()
        c.start()

    local[7].wait()
    remote(recv1.at[0, pl.ds(0, 31)], recv1.at[0, pl.ds(0, 31)], s1s.at[0], s1r.at[0], (g, tp)).wait_recv()
    remote(recv1.at[1], recv1.at[1], s1s.at[1], s1r.at[1], (g, tp)).wait_recv()

    for l in range(2):
        cos8 = cos_t[l * 8:(l + 1) * 8, :][None]
        sin8 = sin_t[l * 8:(l + 1) * 8, :][None]
        for yx in range(16):
            m = recv1[l, yx].astype(F32) + recv1[l, 16 + yx].astype(F32)
            m = m.astype(BF16).astype(F32)
            q = m[:4]
            q = q * cos8 + pltpu.roll(q, 64, 2) * sin8
            for zj in range(4):
                head = (zj // 2) * 32 + yx * 2 + zj % 2
                r0 = l * 512 + head * 8
                qs[r0:r0 + 8, :] = q[zj].astype(BF16).astype(F32)
            yy, xx = yx // 4, yx % 4
            r0 = (l * 4 + yy) * 8
            kvs[r0:r0 + 8, xx * 128:(xx + 1) * 128] = m[4]

    i0 = lax.broadcasted_iota(jnp.int32, (512, 512), 0)
    i1 = lax.broadcasted_iota(jnp.int32, (512, 512), 1)
    target = ((i0 // 32) % 2) * 256 + ((i0 // 64) % 2) * 128 + (i0 // 128) * 32 + i0 % 32
    kvp = dot(kvs[...].astype(BF16), (target == i1).astype(BF16))
    for l in range(2):
        cos8 = cos_t[l * 8:(l + 1) * 8, :]
        sin8 = sin_t[l * 8:(l + 1) * 8, :]
        for yy in range(4):
            r0 = (l * 4 + yy) * 8
            for zz in range(2):
                k = kvp[r0:r0 + 8, zz * 128:(zz + 1) * 128]
                k = k * cos8 + pltpu.roll(k, 64, 1) * sin8
                n = zz * 4 + yy
                knf[l * 8:(l + 1) * 8, n * 128:(n + 1) * 128] = k
                vnf[l * 8:(l + 1) * 8, n * 128:(n + 1) * 128] = kvp[r0:r0 + 8, 256 + zz * 128:256 + (zz + 1) * 128]
    knew = knf[...].astype(BF16)
    vnew = vnf[...].astype(BF16)

    head_of = lax.broadcasted_iota(jnp.int32, (128, 128), 0) % 64
    pos = lax.broadcasted_iota(jnp.int32, (272, 128), 0)
    step = lax.broadcasted_iota(jnp.int32, (272, 128), 1) // 64

    def attend(i, carry):
        l = i // 4
        ii = i % 4
        base = l * 512 + 2 * ii
        q = jnp.concatenate([qs[pl.ds(base + s, 64, stride=8), :] for s in range(2)], axis=0)
        bd = jnp.concatenate(
            [jnp.where(head_of // 8 == n, q, 0.0).astype(BF16) for n in range(8)], axis=1
        )
        keys = jnp.concatenate([pages[pids[i, j], :, :1024] for j in range(4)] + [knew], axis=0)
        values = jnp.concatenate([pages[pids[i, j], :, 1024:] for j in range(4)] + [vnew], axis=0)
        scores = dot_nt(keys, bd) * HEAD_SIZE ** (-0.5)
        first = 256 + 2 * i
        usable = (pos < lens[i]) | (pos == first) | ((pos == first + 1) & (step == 1))
        top = jnp.max(jnp.where(usable, scores, -jnp.inf), axis=0, keepdims=True)
        e = jnp.where(usable, jnp.exp(scores - top), 0.0)
        p = (e / jnp.sum(e, axis=0, keepdims=True)).astype(BF16)
        o = dot_tn(p, values)
        for s in range(2):
            for n in range(8):
                att[pl.ds(pl.multiple_of((2 * i + s) * 64 + n * 8, 8), 8), :] = o[
                    s * 64 + n * 8:s * 64 + (n + 1) * 8, n * 128:(n + 1) * 128
                ]
        return carry

    lax.fori_loop(0, 8, attend, 0, unroll=2)

    def pack2(yx, carry):
        for l in range(2):
            for zj in range(4):
                head = (zj // 2) * 32 + yx * 2 + zj % 2
                send2[l, yx, zj] = att[pl.ds(l * 512 + head, 8, stride=64), :].astype(BF16)
        return carry

    lax.fori_loop(0, 16, pack2, 0)

    def s2_copy(l, o):
        d = (t + o) % 32
        return remote(send2.at[l, d % 16], recv2.at[l, t], s2s.at[l], s2r.at[l], ((g + 4 - l) % 4, d))

    def s2_start(o, carry):
        s2_copy(1, o).start()
        s2_copy(0, o).start()
        return carry

    lax.fori_loop(1, 32, s2_start, 0)
    s2_copy(1, 0).start()
    recv2[0, t] = send2[0, t % 16]

    for a in fw_arrivals(3):
        a.wait_recv()
    remote(recv2.at[0, pl.ds(0, 31)], recv2.at[0, pl.ds(0, 31)], s2s.at[0], s2r.at[0], (g, tp)).wait_recv()
    remote(recv2.at[1], recv2.at[1], s2s.at[1], s2r.at[1], (g, tp)).wait_recv()

    def build(s, carry):
        for l in range(2):
            r0 = pl.multiple_of(l * 256 + s * 16, 16)
            for zj in range(4):
                both = jnp.concatenate([recv2[l, 2 * s + h, zj].astype(F32) for h in range(2)], axis=0)
                lhs[pl.ds(r0, 16), zj * 128:(zj + 1) * 128] = both.astype(BF16)
        return carry

    lax.fori_loop(0, 16, build, 0)

    def partial(oa, ob):
        c0 = pl.multiple_of(slice_index(oa, ob) * 256, 256)
        return dot(lhs[:, :256], wo[0, :, pl.ds(c0, 256)]) + dot(lhs[:, 256:], wo[1, :, pl.ds(c0, 256)])

    def rs_copy(row, kind):
        along_b = 1 if row else 0
        oa = row - 1

        def src(o, rows=None):
            ref = sb.at[oa, o] if along_b else ta.at[o]
            return ref if rows is None else ref.at[pl.ds(rows, 256)]

        halves = rh.at[oa] if along_b else rah
        fulls = rf.at[oa] if along_b else raf
        if kind == 0:
            s, d, way = src(2, 0), halves.at[0], -1
        elif kind == 1:
            s, d, way = src(2, 256), halves.at[1], 1
        elif kind == 2:
            s, d, way = src(3), fulls.at[0], -1
        else:
            s, d, way = src(1), fulls.at[1], 1
        return remote(s, d, rss.at[row, kind], rsr.at[row, kind], near(along_b, way))

    rs = [[rs_copy(row, kind) for kind in range(4)] for row in range(5)]
    order = (2, 1, 3, 0)
    for oa in order:
        sb[oa, 2] = partial(oa, 2).astype(BF16)
        rs[1 + oa][0].start()
        rs[1 + oa][1].start()
    for oa in order:
        sf[oa, 2] = partial(oa, 3)
        rs[1 + oa][0].wait_recv()
        sb[oa, 3, 0:256] = (sf[oa, 2, 0:256] + rh[oa, 0].astype(F32)).astype(BF16)
        sb[oa, 3, 256:512] = sf[oa, 2, 256:512].astype(BF16)
        rs[1 + oa][2].start()
        sf[oa, 1] = partial(oa, 1)
        rs[1 + oa][1].wait_recv()
        sb[oa, 1, 0:256] = sf[oa, 1, 0:256].astype(BF16)
        sb[oa, 1, 256:512] = (sf[oa, 1, 256:512] + rh[oa, 1].astype(F32)).astype(BF16)
        rs[1 + oa][3].start()
    for oa in order:
        sf[oa, 0] = partial(oa, 0)

    def total(oa):
        rs[1 + oa][2].wait_recv()
        rs[1 + oa][3].wait_recv()
        return sf[oa, 0] + rf[oa, 0].astype(F32) + rf[oa, 1].astype(F32)

    ta[2] = total(2).astype(BF16)
    rs[0][0].start()
    rs[0][1].start()
    sf[1, 0] = total(1)
    rs[0][1].wait_recv()
    ta[1, 0:256] = sf[1, 0, 0:256].astype(BF16)
    ta[1, 256:512] = (sf[1, 0, 256:512] + rah[1].astype(F32)).astype(BF16)
    rs[0][3].start()
    sf[3, 0] = total(3)
    rs[0][0].wait_recv()
    ta[3, 0:256] = (sf[3, 0, 0:256] + rah[0].astype(F32)).astype(BF16)
    ta[3, 256:512] = sf[3, 0, 256:512].astype(BF16)
    rs[0][2].start()
    sf[0, 0] = total(0)
    rs[0][2].wait_recv()
    rs[0][3].wait_recv()
    final = (sf[0, 0] + raf[0].astype(F32) + raf[1].astype(F32)).astype(BF16)
    out[...] = dot(back[...], final).astype(BF16)

    for row in range(5):
        for kind in range(4):
            ag[row][kind].wait_send()
            rs[row][kind].wait_send()
    for i in range(4):
        for c in wx_copies(i) + fw_copies(i):
            c.wait_send()
    remote(lowrecv.at[pl.ds(0, 31)], lowrecv.at[pl.ds(0, 31)], lows, lowr, (g, tp)).wait_send()
    remote(screcv.at[pl.ds(0, 31)], screcv.at[pl.ds(0, 31)], scs, scr, (g, tp)).wait_send()
    remote(recv1.at[0, pl.ds(0, 31)], recv1.at[0, pl.ds(0, 31)], s1s.at[0], s1r.at[0], (g, tp)).wait_send()
    remote(recv1.at[1], recv1.at[1], s1s.at[1], s1r.at[1], (g, tp)).wait_send()
    remote(recv2.at[0, pl.ds(0, 31)], recv2.at[0, pl.ds(0, 31)], s2s.at[0], s2r.at[0], (g, tp)).wait_send()
    remote(recv2.at[1], recv2.at[1], s2s.at[1], s2r.at[1], (g, tp)).wait_send()


def scratch():
    v = pltpu.VMEM
    dma = pltpu.SemaphoreType.DMA
    return [
        v((4, 4, 512, 256), BF16),
        v((4096, 256), BF16),
        v((4096, 256), BF16),
        v((128, 4096), BF16),
        v((2, 256, 4096), BF16),
        v((32, 64, 2048), BF16),
        v((32, 256, 128), BF16),
        v((2048, 256), BF16),
        v((1024, 64), BF16),
        v((16, 128), F32),
        v((16, 128), F32),
        pltpu.SMEM((8,), jnp.int32),
        pltpu.SMEM((8, 4), jnp.int32),
        v((512, 512), BF16),
        v((512, 640), F32),
        v((512, 256), F32),
        v((32, 2, 8, 128), BF16),
        v((32, 2, 8, 128), BF16),
        v((2, 8, 128), BF16),
        v((32, 2, 8, 128), BF16),
        v((512, 256), F32),
        v((512, 128), F32),
        v((2, 32, 5, 8, 128), BF16),
        v((2, 32, 5, 8, 128), BF16),
        v((1024, 128), F32),
        v((64, 512), F32),
        v((16, 1024), F32),
        v((16, 1024), F32),
        v((1024, 128), F32),
        v((2, 16, 4, 8, 128), BF16),
        v((2, 32, 4, 8, 128), BF16),
        v((512, 512), BF16),
        v((4, 4, 512, 256), BF16),
        v((4, 3, 512, 256), F32),
        v((4, 2, 256, 256), BF16),
        v((4, 2, 512, 256), BF16),
        v((4, 512, 256), BF16),
        v((2, 256, 256), BF16),
        v((2, 512, 256), BF16),
        dma((8,)),
        dma((5, 4)), dma((5, 4)),
        dma((4, 2)), dma((4, 2)),
        dma((4, 2)), dma((4, 2)),
        dma, dma, dma, dma,
        dma((2,)), dma((2,)),
        dma((2,)), dma((2,)),
        dma((5, 4)), dma((5, 4)),
        pltpu.SemaphoreType.REGULAR,
        pltpu.SemaphoreType.REGULAR,
    ]


def local(
    hidden, query_weight, key_weight, value_weight, output_weight, adapter_down_maps,
    adapter_up_query, adapter_up_value, key_value_pages, row_adapter_index,
    row_rank_bucket, lengths, row_page_index,
):
    positions = np.arange(264, dtype=np.float32)
    inverse_freq = np.exp(np.float32(-math.log(ROPE_BASE)) * np.arange(64, dtype=np.float32) / np.float32(64))
    angles = positions[:, None] * np.concatenate([inverse_freq, inverse_freq])[None].astype(np.float32)
    sign = np.where(np.arange(128) < 64, -1.0, 1.0)[None]
    cos_tab = jnp.asarray(np.cos(angles), F32)
    sin_tab = jnp.asarray(np.sin(angles) * sign, F32)

    vm = pl.BlockSpec(memory_space=pltpu.VMEM)
    sm = pl.BlockSpec(memory_space=pltpu.SMEM)
    hbm = pl.BlockSpec(memory_space=pl.ANY)
    res = pl.pallas_call(
        kernel,
        out_shape=jax.ShapeDtypeStruct((TOKENS, 256), BF16),
        in_specs=[vm] * 6 + [sm] * 2 + [hbm] * 8,
        out_specs=vm,
        scratch_shapes=scratch(),
        compiler_params=pltpu.CompilerParams(
            collective_id=0, has_side_effects=True, vmem_limit_bytes=60 * 1024 * 1024
        ),
    )(
        hidden.reshape(TOKENS, 256), row_adapter_index[None, :], row_rank_bucket[None, :], row_page_index.T,
        cos_tab, sin_tab, lengths, row_page_index.T,
        query_weight, key_weight.T, value_weight.T, output_weight, adapter_down_maps,
        adapter_up_query.reshape(2048, 256),
        adapter_up_value.transpose(0, 2, 1).reshape(1024, 64), key_value_pages,
    )
    return res.reshape(256, STEPS, 256)


def solution(mesh):
    in_specs = (
        P("group", None, "tensor"),
        P(None, "tensor"),
        P(None, "tensor"),
        P(None, "tensor"),
        P("tensor", None),
        P(None, "tensor", None),
        P(None, None, "tensor"),
        P(None, None, "tensor"),
        P(("group", "tensor"), None, None),
        P("group"),
        P("group"),
        P(),
        P(),
    )
    out_specs = P("group", None, "tensor")
    return jax.shard_map(local, mesh=mesh, in_specs=in_specs, out_specs=out_specs, check_vma=False)
```

```python
import functools
import math

import jax
import jax.numpy as jnp
import numpy as np
from jax import lax
from jax.experimental import pallas as pl
from jax.experimental.pallas import tpu as pltpu
from jax.sharding import PartitionSpec as P

QUERY_HEADS = 64
KEY_VALUE_HEADS = 8
HEAD_SIZE = 128
RANK_LIMIT = 64
ADAPTERS = 32
STEPS = 2
RES = 4
ROWS_DEV = 8
TOKENS = 512
POOL = 32
ROPE_BASE = 500000.0
MESH = pl.DeviceIdType.MESH
F32 = jnp.float32
BF16 = jnp.bfloat16


def dot(a, b):
    return jnp.dot(a, b, preferred_element_type=F32)


def dot_nt(a, b):
    return lax.dot_general(a, b, (((1,), (1,)), ((), ())), preferred_element_type=F32)


def dot_tn(a, b):
    return lax.dot_general(a, b, (((0,), (0,)), ((), ())), preferred_element_type=F32)


def remote(src, dst, send, recv, device):
    return pltpu.make_async_remote_copy(
        src_ref=src, dst_ref=dst, send_sem=send, recv_sem=recv,
        device_id=device, device_id_type=MESH,
    )


def kernel(
    hid, adapters, buckets, table_v, cos_tab, sin_tab, lengths, table,
    qw, kt, vt, ow, down, upq, upv, pool,
    out,
    hb, wq, wqp, kvt, wo, pages, dn, uq, uv,
    cos_t, sin_t, lens, pids, back,
    acc, metap, lowsend, lowrecv, scown, screcv, lift, liftv,
    send1, recv1, qs, kvs, knf, vnf, att, send2, recv2, lhs,
    sb, rh, rf, ta, ta0, rah, raf, kvperm,
    loc, ags, agr, wxs, wxr, fws, fwr, lows, lowr, scs, scr, s1s, s1r, s2s, s2r, rss, rsr, plane_sem, all_sem,
):
    g = lax.axis_index("group")
    t = lax.axis_index("tensor")
    core = g % 2
    z = t // 16
    y = (t // 4) % 4
    x = t % 4
    zp = 1 - z
    tp = zp * 16 + y * 4 + x
    g2 = (g + 2) % 4
    gs = g + 1 - 2 * core

    def near(along_b, d):
        on_x = (1 - core) * (1 - along_b) + core * along_b
        on_y = 1 - on_x
        xx = (x + 4 + d * on_x) % 4
        yy = (y + 4 + d * on_y) % 4
        return (g, z * 16 + yy * 4 + xx)

    def slice_index(oa, ob):
        dx = oa * (1 - core) + ob * core
        dy = oa * core + ob * (1 - core)
        return ((y + dy) % 4) * 4 + (x + dx) % 4

    half = z * 4096
    local = [
        (qw.at[pl.ds(pl.multiple_of(half, 4096), 4096)], wq),
        (kt.at[:, pl.ds(pl.multiple_of(half, 4096), 4096)], kvt.at[pl.ds(pl.multiple_of(z * 64, 32), 32)]),
        (vt.at[:, pl.ds(pl.multiple_of(half, 4096), 4096)], kvt.at[pl.ds(pl.multiple_of(z * 64 + 32, 32), 32)]),
        (ow.at[:, pl.ds(pl.multiple_of(half, 4096), 4096)], wo.at[z]),
        (down, dn),
        (upq, uq),
        (upv, uv),
        (pool, pages),
    ]
    local = [pltpu.make_async_copy(s, d, loc.at[i]) for i, (s, d) in enumerate(local)]
    for i in (4, 0, 1, 2, 5, 6, 3, 7):
        local[i].start()

    barrier = pltpu.get_barrier_semaphore()

    def ring_x(d):
        return (g, z * 16 + y * 4 + (x + d) % 4)

    def ring_y(d):
        return (g, z * 16 + ((y + d) % 4) * 4 + x)

    def line_z(d):
        zz = (2 * (g // 2) + z + d // 2) % 4
        return ((zz // 2) * 2 + (core + d) % 2, (zz % 2) * 16 + y * 4 + x)

    def greet(sem, device):
        pl.semaphore_signal(sem, inc=1, device_id=device, device_id_type=MESH)

    for d in range(1, 4):
        greet(barrier, ring_x(d))
        greet(barrier, ring_y(d))
    for d in range(1, 8):
        greet(barrier, line_z(d))

    def iota(shape, dim):
        return lax.broadcasted_iota(jnp.int32, shape, dim)

    tok = iota((8, TOKENS), 1)
    spread = (iota((256, TOKENS), 0) == iota((256, TOKENS), 1) // 2).astype(BF16)
    ahead = (
        (iota((256, TOKENS), 0) // 8 == iota((256, TOKENS), 1) // 16)
        & (iota((256, TOKENS), 0) < iota((256, TOKENS), 1) // 2)
    ).astype(BF16)
    first_page = table_v[0:1, pl.ds(pl.multiple_of(g * 256, 256), 256)]
    moved = (first_page // POOL != g * 32 + iota((1, 256), 1) // 8).astype(F32)
    moved = jnp.broadcast_to(moved, (8, 256)).astype(BF16)
    resumed = dot(moved, spread).astype(jnp.int32)
    before = dot(moved, ahead).astype(jnp.int32)
    place = jnp.where(resumed == 1, before, (tok // 2) % 8 - before)
    pos = resumed * 256 + (tok // 16) * 8 + place * 2 + tok % 2
    perm = (iota((TOKENS, TOKENS), 0) == pos[0:1]).astype(BF16)
    mine = dot(perm, hid[...].reshape(TOKENS, 256)).astype(BF16)
    for h in range(2):
        hb[h, 0, 0] = mine[h * 256:(h + 1) * 256]

    def ag_copy(h, row, kind):
        along_b = 1 if row else 0
        oa = row - 1

        def at(o, rows=None):
            ref = hb.at[h, oa, o] if along_b else hb.at[h, o, 0]
            return ref if rows is None else ref.at[pl.ds(rows, 128)]

        if kind == 0:
            src, dst, d = at(0), at(1), -1
        elif kind == 1:
            src, dst, d = at(0), at(3), 1
        elif kind == 2:
            src, dst, d = at(1, 0), at(2, 0), -1
        else:
            src, dst, d = at(3, 128), at(2, 128), 1
        return remote(src, dst, ags.at[h, row, kind], agr.at[h, row, kind], near(along_b, d))

    ag = [[[ag_copy(h, row, kind) for kind in range(4)] for row in range(5)] for h in range(2)]

    def arrive(h, row, kind):
        ag[h][row][kind].wait_recv()

    def own(h):
        for row in (0, 1):
            for kind in (0, 1):
                ag[h][row][kind].start()

    def first_ring(h):
        arrive(h, 0, 0)
        ag[h][0][2].start()
        ag[h][2][0].start()
        ag[h][2][1].start()
        arrive(h, 0, 1)
        ag[h][0][3].start()
        ag[h][4][0].start()
        ag[h][4][1].start()
        forward(h, 0)

    def forward(h, oa):
        for kind in (0, 1):
            arrive(h, 1 + oa, kind)
            ag[h][1 + oa][kind + 2].start()

    def first_ring_far(h):
        arrive(h, 0, 2)
        arrive(h, 0, 3)
        ag[h][3][0].start()
        ag[h][3][1].start()

    def along(row):
        wide = jnp.broadcast_to(row.astype(F32), (128, 256)).astype(BF16)
        return dot_nt(perm, dot(wide, spread).astype(BF16))

    metap[:, :128] = along(adapters[...])
    lane = iota((TOKENS, 128), 1)
    idxi = metap[:, :128].astype(jnp.int32)

    local[4].wait()

    def low_part(first, count):
        total = None
        for a in range(first, first + count, 2):
            maps = jnp.concatenate([dn[a], dn[a + 1]], axis=1)
            part = jnp.concatenate([dot(hb[h, 0, 0], maps) for h in range(2)], axis=0)
            part = jnp.where(idxi == a, part[:, :128], 0.0) + jnp.where(idxi == a + 1, part[:, 128:], 0.0)
            total = part if total is None else total + part
        return total

    low = low_part(0, ADAPTERS)
    for l in range(2):
        lowsend[:, l] = low[l * 256:(l + 1) * 256].reshape(32, 8, 128).astype(BF16)
    metap[:, 128:] = along(buckets[...])

    pl.semaphore_wait(barrier, 13)
    own(0)
    for d in range(1, 4):
        greet(plane_sem, ring_y(d))

    def wx_pieces(zq, q, zd):
        c0 = pl.multiple_of(zd * 4096 + q * 1024, 1024)
        d0 = pl.multiple_of(q * 1024, 1024)
        r0 = pl.multiple_of(q * 64, 64)
        return [
            (qw.at[pl.ds(c0, 1024)], wqp.at[pl.ds(d0, 1024)]),
            (kt.at[:, pl.ds(c0, 1024)], kvt.at[pl.ds(pl.multiple_of(zq * 64, 32), 32), pl.ds(d0, 1024)]),
            (vt.at[:, pl.ds(c0, 1024)], kvt.at[pl.ds(pl.multiple_of(zq * 64 + 32, 32), 32), pl.ds(d0, 1024)]),
            (ow.at[pl.ds(r0, 64), pl.ds(pl.multiple_of(zd * 4096, 4096), 4096)], wo.at[zq, pl.ds(r0, 64)]),
        ]

    def wx_copies(i):
        s, d = wx_pieces(z, g, zp)[i]
        return [remote(s, d, wxs.at[i, j], wxr.at[i, j], (gd, tp)) for j, gd in enumerate((g, g2))]

    def wx_arrivals(i):
        res = []
        for j, q in enumerate((g, g2)):
            s, d = wx_pieces(zp, q, z)[i]
            res.append(remote(s, d, wxs.at[i, j], wxr.at[i, j], (g, tp)))
        return res

    def fw_copies(i):
        res = []
        for j, q in enumerate((g, g2)):
            _, d = wx_pieces(zp, q, z)[i]
            res.append(remote(d, d, fws.at[i, j], fwr.at[i, j], (gs, t)))
        return res

    def fw_arrivals(i):
        res = []
        for j, q in enumerate((gs, (gs + 2) % 4)):
            _, d = wx_pieces(zp, q, z)[i]
            res.append(remote(d, d, fws.at[i, j], fwr.at[i, j], (gs, t)))
        return res

    for i in range(3):
        for c in wx_copies(i):
            c.start()
    own(1)

    def low_copy(o):
        d = (t + o) % 32
        return remote(lowsend.at[d], lowrecv.at[t], lows, lowr, (g, d))

    def low_start(o, carry):
        low_copy(o).start()
        return carry

    pl.semaphore_wait(plane_sem, 3)
    for d in range(1, 8):
        greet(all_sem, line_z(d))
    first_ring(0)
    pl.semaphore_wait(all_sem, 7)
    lax.fori_loop(1, 32, low_start, 0)
    lowrecv[t] = lowsend[t]
    first_ring(1)
    first_ring_far(0)
    forward(0, 1)
    forward(0, 3)

    remote(lowrecv.at[pl.ds(0, 31)], lowrecv.at[pl.ds(0, 31)], lows, lowr, (g, tp)).wait_recv()
    lane16 = lax.broadcasted_iota(jnp.int32, (8, 128), 1) % RANK_LIMIT
    for l in range(2):
        lowrank = jnp.sum(lowrecv[:, l].astype(F32), axis=0)
        bucket = metap[pl.ds(pl.multiple_of(l * 256 + t * 8, 8), 8), 128:]
        scaled = jnp.where(lane16.astype(F32) < bucket, lowrank * (0.5 * RANK_LIMIT) / bucket, 0.0)
        scown[l] = scaled.astype(BF16)

    def sc_copy(o):
        d = (t + o) % 32
        return remote(scown, screcv.at[t], scs, scr, (g, d))

    def sc_start(o, carry):
        sc_copy(o).start()
        return carry

    lax.fori_loop(1, 32, sc_start, 0)
    screcv[t] = scown[...]

    first_ring_far(1)
    forward(0, 2)
    forward(1, 1)
    forward(1, 3)
    base = (g * 32 + t) * POOL
    for l in range(2):
        gg = (g + 4 - l) % 4
        first = gg * 256 + t * ROWS_DEV
        marks, spots = [], []
        count = jnp.int32(0)
        for k in range(ROWS_DEV):
            mark = jnp.where(table[0, first + k] // POOL != gg * 32 + t, 1, 0)
            marks.append(mark)
            spots.append(jnp.where(mark == 1, count, k - count))
            count = count + mark
        for i in range(RES):
            mine = [(marks[k] == l) & (spots[k] == i) for k in range(ROWS_DEV)]
            row = l * RES + i
            lens[row] = sum(jnp.where(mine[k], lengths[first + k], 0) for k in range(ROWS_DEV))
            for j in range(4):
                page = sum(jnp.where(mine[k], table[j, first + k], 0) for k in range(ROWS_DEV))
                pids[row, j] = jnp.clip(page - base, 0, POOL - 1)
            cos_t[2 * row:2 * row + 2, :] = cos_tab[pl.ds(lens[row], 2), :]
            sin_t[2 * row:2 * row + 2, :] = sin_tab[pl.ds(lens[row], 2), :]

    eye = (iota((TOKENS, TOKENS), 0) == iota((TOKENS, TOKENS), 1)).astype(BF16)
    back[...] = dot_nt(eye, perm).astype(BF16)
    i0 = iota((512, 512), 0)
    target = ((i0 // 32) % 2) * 256 + ((i0 // 64) % 2) * 128 + (i0 // 128) * 32 + i0 % 32
    kvperm[...] = (target == iota((512, 512), 1)).astype(BF16)

    for i in (0, 1, 2):
        local[i].wait()
        for a, c in zip(wx_arrivals(i), fw_copies(i)):
            a.wait_recv()
            c.start()
    for c in wx_copies(3):
        c.start()
    forward(1, 2)

    remote(screcv.at[pl.ds(0, 31)], screcv.at[pl.ds(0, 31)], scs, scr, (g, tp)).wait_recv()
    local[5].wait()
    local[6].wait()
    sc = jnp.concatenate([screcv[:, l].astype(F32).reshape(256, 128) for l in range(2)], axis=0)
    swapped = pltpu.roll(sc, 64, 1)
    sq = jnp.where(lane < 64, sc, swapped)
    svk = jnp.where(lane < 64, swapped, 0.0).astype(BF16)[:, :64]
    lift[...] = jnp.zeros(lift.shape, F32)

    def lift_step(j, carry):
        two = [jnp.where(idxi == 4 * j + 2 * e + lane // 64, sq, 0.0).astype(BF16) for e in range(2)]
        lift[...] = lift[...] + dot(jnp.concatenate(two, axis=1), uq[pl.ds(pl.multiple_of(j * 256, 256), 256)])
        return carry

    lax.fori_loop(0, ADAPTERS // 4, lift_step, 0, unroll=2)
    liftv[...] = jnp.zeros(liftv.shape, F32)
    def liftv_step(j, carry):
        part = dot_nt(svk, uv[pl.ds(pl.multiple_of(j * 128, 128), 128)])
        liftv[...] = liftv[...] + jnp.where(idxi == 4 * j + lane // 32, part, 0.0)
        return carry

    lax.fori_loop(0, ADAPTERS // 4, liftv_step, 0, unroll=2)
    lv = liftv[...]
    lv = lv + pltpu.roll(lv, 64, 1)
    lv = lv + pltpu.roll(lv, 32, 1)
    place = lane // 32 == 2 * z + 1
    liftv[...] = jnp.where(place, lv, 0.0)
    for i in (0, 1, 2):
        for a in fw_arrivals(i):
            a.wait_recv()
    acc[...] = jnp.zeros(acc.shape, F32)

    def project(h, oa, ob):
        k0 = pl.multiple_of(slice_index(oa, ob) * 256, 256)
        x_in = hb[h, oa, ob]
        rows = slice(h * 256, (h + 1) * 256)
        acc[rows, 0:256] = acc[rows, 0:256] + dot(x_in, wq[pl.ds(k0, 256)])
        acc[rows, 256:512] = acc[rows, 256:512] + dot(x_in, wqp[pl.ds(k0, 256)])
        acc[rows, 512:640] = acc[rows, 512:640] + dot_nt(x_in, kvt[:, pl.ds(k0, 256)])


    def message(l, v, block):
        send1[l, :, block] = v.reshape(32, 8, 128).astype(BF16)

    def s1_copy(l, o):
        d = (t + o) % 32
        return remote(send1.at[l, d], recv1.at[l, t], s1s.at[l], s1r.at[l], ((g + l) % 4, d))

    def project_near(h):
        for oa in range(4):
            project(h, oa, 0)
        for oa in (0, 1, 3, 2):
            project(h, oa, 1)
            project(h, oa, 3)

    def project_far(h):
        for oa in (0, 1, 3, 2):
            arrive(h, 1 + oa, 2)
            arrive(h, 1 + oa, 3)
            project(h, oa, 2)

    def scatter_rows(l):
        rows = slice(l * 256, (l + 1) * 256)
        for j in range(2):
            message(l, acc[rows, j * 128:(j + 1) * 128] + lift[rows, j * 128:(j + 1) * 128], 2 * z + j)
            message(l, acc[rows, 256 + j * 128:256 + (j + 1) * 128], 2 * zp + j)
        message(l, acc[rows, 512:640] + liftv[rows, :], 4)

        def start(o, carry):
            s1_copy(l, o).start()
            return carry

        lax.fori_loop(1, 32, start, 0)
        if l == 0:
            recv1[0, t] = send1[0, t]
        else:
            s1_copy(1, 0).start()

    def rows_arrive(recv, send_sem, recv_sem, l):
        ref = recv.at[0, pl.ds(0, 31)] if l == 0 else recv.at[1]
        return remote(ref, ref, send_sem.at[l], recv_sem.at[l], (g, tp))

    head_of = iota((128, 128), 0) % 64
    cache_pos = iota((272, 128), 0)
    step = iota((272, 128), 1) // 64

    def attend(l):
        cos8 = cos_t[l * 8:(l + 1) * 8, :]
        sin8 = sin_t[l * 8:(l + 1) * 8, :]
        for yx in range(16):
            m = recv1[l, yx].astype(F32) + recv1[l, 16 + yx].astype(F32)
            m = m.astype(BF16).astype(F32)
            q = m[:4]
            q = q * cos8[None] + pltpu.roll(q, 64, 2) * sin8[None]
            for zj in range(4):
                head = (zj // 2) * 32 + yx * 2 + zj % 2
                r0 = l * 512 + head * 8
                qs[r0:r0 + 8, :] = q[zj].astype(BF16).astype(F32)
            yy, xx = yx // 4, yx % 4
            r0 = (l * 4 + yy) * 8
            kvs[r0:r0 + 8, xx * 128:(xx + 1) * 128] = m[4]
        kvp = dot(kvs[l * 32:(l + 1) * 32, :].astype(BF16), kvperm[...])
        for yy in range(4):
            r0 = yy * 8
            for zz in range(2):
                k = kvp[r0:r0 + 8, zz * 128:(zz + 1) * 128]
                k = k * cos8 + pltpu.roll(k, 64, 1) * sin8
                n = zz * 4 + yy
                knf[l, 0:8, n * 128:(n + 1) * 128] = k
                vnf[l, 0:8, n * 128:(n + 1) * 128] = kvp[r0:r0 + 8, 256 + zz * 128:256 + (zz + 1) * 128]
        knf[l, 8:16, :] = jnp.zeros((8, 1024), F32)
        vnf[l, 8:16, :] = jnp.zeros((8, 1024), F32)
        knew = knf[l].astype(BF16)
        vnew = vnf[l].astype(BF16)

        for ii in range(RES):
            i = l * RES + ii
            q = jnp.concatenate(
                [qs[pl.ds(l * 512 + 2 * ii + st, 64, stride=8), :] for st in range(2)], axis=0
            )
            bd = jnp.concatenate(
                [jnp.where(head_of // 8 == n, q, 0.0).astype(BF16) for n in range(8)], axis=1
            )
            keys = jnp.concatenate([pages[pids[i, j], :, :1024] for j in range(4)] + [knew], axis=0)
            values = jnp.concatenate([pages[pids[i, j], :, 1024:] for j in range(4)] + [vnew], axis=0)
            scores = dot_nt(keys, bd) * HEAD_SIZE ** (-0.5)
            first = 256 + 2 * ii
            usable = (
                (cache_pos < lens[i])
                | (cache_pos == first)
                | ((cache_pos == first + 1) & (step == 1))
            )
            top = jnp.max(jnp.where(usable, scores, -jnp.inf), axis=0, keepdims=True)
            e = jnp.where(usable, jnp.exp(scores - top), 0.0)
            probs = (e / jnp.sum(e, axis=0, keepdims=True)).astype(BF16)
            o = dot_tn(probs, values)
            for st in range(2):
                for n in range(8):
                    r0 = (2 * i + st) * 64 + n * 8
                    att[r0:r0 + 8, :] = o[st * 64 + n * 8:st * 64 + (n + 1) * 8, n * 128:(n + 1) * 128]

        def pack(yx, carry):
            for zj in range(4):
                head = (zj // 2) * 32 + yx * 2 + zj % 2
                send2[l, yx, zj] = att[pl.ds(l * 512 + head, 8, stride=64), :].astype(BF16)
            return carry

        lax.fori_loop(0, 16, pack, 0, unroll=4)

    def s2_copy(l, o):
        d = (t + o) % 32
        return remote(send2.at[l, d % 16], recv2.at[l, t], s2s.at[l], s2r.at[l], ((g + 4 - l) % 4, d))

    def scatter_heads(l):
        def start(o, carry):
            s2_copy(l, o).start()
            return carry

        lax.fori_loop(1, 32, start, 0)
        if l == 0:
            recv2[0, t] = send2[0, t % 16]
        else:
            s2_copy(1, 0).start()

    def build(l):
        rows_arrive(recv2, s2s, s2r, l).wait_recv()

        def some(k, carry):
            r0 = pl.multiple_of(l * 256 + k * 16, 16)
            for zj in range(4):
                both = jnp.concatenate([recv2[l, 2 * k + e, zj].astype(F32) for e in range(2)], axis=0)
                lhs[pl.ds(r0, 16), zj * 128:(zj + 1) * 128] = both.astype(BF16)
            return carry

        lax.fori_loop(0, 16, some, 0, unroll=4)

    def partial(h, oa, ob):
        c0 = pl.multiple_of(slice_index(oa, ob) * 256, 256)
        rows = slice(h * 256, (h + 1) * 256)
        return dot(lhs[rows, :256], wo[0, :, pl.ds(c0, 256)]) + dot(lhs[rows, 256:], wo[1, :, pl.ds(c0, 256)])

    def rs_copy(h, row, kind):
        along_b = 1 if row else 0
        oa = row - 1

        def src(o, rows=None):
            ref = sb.at[h, oa, o] if along_b else ta.at[h, o]
            return ref if rows is None else ref.at[pl.ds(rows, 128)]

        halves = rh.at[h, oa] if along_b else rah.at[h]
        fulls = rf.at[h, oa] if along_b else raf.at[h]
        if kind == 0:
            s, d, way = src(2, 0), halves.at[0], -1
        elif kind == 1:
            s, d, way = src(2, 128), halves.at[1], 1
        elif kind == 2:
            s, d, way = src(3), fulls.at[0], -1
        else:
            s, d, way = src(1), fulls.at[1], 1
        return remote(s, d, rss.at[h, row, kind], rsr.at[h, row, kind], near(along_b, way))

    rs = [[[rs_copy(h, row, kind) for kind in range(4)] for row in range(5)] for h in range(2)]
    order = (2, 1, 3, 0)

    def reduce_far(h):
        for oa in order:
            sb[h, oa, 2] = partial(h, oa, 2).astype(BF16)
            rs[h][1 + oa][0].start()
            rs[h][1 + oa][1].start()

    def reduce_near(h):
        for oa in order:
            part = partial(h, oa, 3)
            rs[h][1 + oa][0].wait_recv()
            sb[h, oa, 3, 0:128] = (part[0:128] + rh[h, oa, 0].astype(F32)).astype(BF16)
            sb[h, oa, 3, 128:256] = part[128:256].astype(BF16)
            rs[h][1 + oa][2].start()
            part = partial(h, oa, 1)
            rs[h][1 + oa][1].wait_recv()
            sb[h, oa, 1, 0:128] = part[0:128].astype(BF16)
            sb[h, oa, 1, 128:256] = (part[128:256] + rh[h, oa, 1].astype(F32)).astype(BF16)
            rs[h][1 + oa][3].start()

    def total(h, oa):
        part = partial(h, oa, 0)
        rs[h][1 + oa][2].wait_recv()
        rs[h][1 + oa][3].wait_recv()
        return part + rf[h, oa, 0].astype(F32) + rf[h, oa, 1].astype(F32)

    def reduce_first(h):
        ta[h, 2] = total(h, 2).astype(BF16)
        rs[h][0][0].start()
        rs[h][0][1].start()

    def reduce_last(h):
        part = total(h, 1)
        rs[h][0][1].wait_recv()
        ta[h, 1, 0:128] = part[0:128].astype(BF16)
        ta[h, 1, 128:256] = (part[128:256] + rah[h, 1].astype(F32)).astype(BF16)
        rs[h][0][3].start()
        part = total(h, 3)
        rs[h][0][0].wait_recv()
        ta[h, 3, 0:128] = (part[0:128] + rah[h, 0].astype(F32)).astype(BF16)
        ta[h, 3, 128:256] = part[128:256].astype(BF16)
        rs[h][0][2].start()
        ta0[h] = total(h, 0)

    def result(h):
        rs[h][0][2].wait_recv()
        rs[h][0][3].wait_recv()
        return (ta0[h] + raf[h, 0].astype(F32) + raf[h, 1].astype(F32)).astype(BF16)

    project_near(0)
    project_far(0)
    scatter_rows(0)
    project_near(1)
    project_far(1)
    scatter_rows(1)
    local[7].wait()
    rows_arrive(recv1, s1s, s1r, 0).wait_recv()
    attend(0)
    scatter_heads(0)
    rows_arrive(recv1, s1s, s1r, 1).wait_recv()
    attend(1)
    scatter_heads(1)
    local[3].wait()
    for a, c in zip(wx_arrivals(3), fw_copies(3)):
        a.wait_recv()
        c.start()
    for a in fw_arrivals(3):
        a.wait_recv()
    build(0)
    reduce_far(0)
    reduce_near(0)
    build(1)
    reduce_far(1)
    reduce_first(0)
    reduce_last(0)
    reduce_near(1)
    reduce_first(1)
    reduce_last(1)
    low_half = result(0)
    final = jnp.concatenate([low_half, result(1)], axis=0)
    out[...] = dot(back[...], final).astype(BF16).reshape(256, STEPS, 256)

    for h in range(2):
        for row in range(5):
            for kind in range(4):
                ag[h][row][kind].wait_send()
                rs[h][row][kind].wait_send()
    for i in range(4):
        for c in wx_copies(i) + fw_copies(i):
            c.wait_send()
    remote(lowrecv.at[pl.ds(0, 31)], lowrecv.at[pl.ds(0, 31)], lows, lowr, (g, tp)).wait_send()
    remote(screcv.at[pl.ds(0, 31)], screcv.at[pl.ds(0, 31)], scs, scr, (g, tp)).wait_send()
    for l in range(2):
        rows_arrive(recv1, s1s, s1r, l).wait_send()
        rows_arrive(recv2, s2s, s2r, l).wait_send()


def scratch():
    v = pltpu.VMEM
    dma = pltpu.SemaphoreType.DMA
    return [
        v((2, 4, 4, 256, 256), BF16),
        v((4096, 256), BF16),
        v((4096, 256), BF16),
        v((128, 4096), BF16),
        v((2, 256, 4096), BF16),
        v((32, 64, 2048), BF16),
        v((32, 256, 128), BF16),
        v((2048, 256), BF16),
        v((1024, 64), BF16),
        v((16, 128), F32),
        v((16, 128), F32),
        pltpu.SMEM((8,), jnp.int32),
        pltpu.SMEM((8, 4), jnp.int32),
        v((512, 512), BF16),
        v((512, 640), F32),
        v((512, 256), F32),
        v((32, 2, 8, 128), BF16),
        v((32, 2, 8, 128), BF16),
        v((2, 8, 128), BF16),
        v((32, 2, 8, 128), BF16),
        v((512, 256), F32),
        v((512, 128), F32),
        v((2, 32, 5, 8, 128), BF16),
        v((2, 32, 5, 8, 128), BF16),
        v((1024, 128), F32),
        v((64, 512), F32),
        v((2, 16, 1024), F32),
        v((2, 16, 1024), F32),
        v((1024, 128), F32),
        v((2, 16, 4, 8, 128), BF16),
        v((2, 32, 4, 8, 128), BF16),
        v((512, 512), BF16),
        v((2, 4, 4, 256, 256), BF16),
        v((2, 4, 2, 128, 256), BF16),
        v((2, 4, 2, 256, 256), BF16),
        v((2, 4, 256, 256), BF16),
        v((2, 256, 256), F32),
        v((2, 2, 128, 256), BF16),
        v((2, 2, 256, 256), BF16),
        v((512, 512), BF16),
        dma((8,)),
        dma((2, 5, 4)), dma((2, 5, 4)),
        dma((4, 2)), dma((4, 2)),
        dma((4, 2)), dma((4, 2)),
        dma, dma, dma, dma,
        dma((2,)), dma((2,)),
        dma((2,)), dma((2,)),
        dma((2, 5, 4)), dma((2, 5, 4)),
        pltpu.SemaphoreType.REGULAR,
        pltpu.SemaphoreType.REGULAR,
    ]


def local(
    hidden, query_weight, key_weight, value_weight, output_weight, adapter_down_maps,
    adapter_up_query, adapter_up_value, key_value_pages, row_adapter_index,
    row_rank_bucket, lengths, row_page_index,
):
    positions = np.arange(264, dtype=np.float32)
    inverse_freq = np.exp(np.float32(-math.log(ROPE_BASE)) * np.arange(64, dtype=np.float32) / np.float32(64))
    angles = positions[:, None] * np.concatenate([inverse_freq, inverse_freq])[None].astype(np.float32)
    sign = np.where(np.arange(128) < 64, -1.0, 1.0)[None]
    cos_tab = jnp.asarray(np.cos(angles), F32)
    sin_tab = jnp.asarray(np.sin(angles) * sign, F32)

    vm = pl.BlockSpec(memory_space=pltpu.VMEM)
    sm = pl.BlockSpec(memory_space=pltpu.SMEM)
    hbm = pl.BlockSpec(memory_space=pl.ANY)
    res = pl.pallas_call(
        kernel,
        out_shape=jax.ShapeDtypeStruct((256, STEPS, 256), BF16),
        in_specs=[vm] * 6 + [sm] * 2 + [hbm] * 8,
        out_specs=vm,
        scratch_shapes=scratch(),
        compiler_params=pltpu.CompilerParams(
            collective_id=0, has_side_effects=True, vmem_limit_bytes=60 * 1024 * 1024
        ),
    )(
        hidden, row_adapter_index[None, :], row_rank_bucket[None, :], row_page_index.T,
        cos_tab, sin_tab, lengths, row_page_index.T,
        query_weight, key_weight.T, value_weight.T, output_weight, adapter_down_maps,
        adapter_up_query.reshape(2048, 256),
        adapter_up_value.transpose(0, 2, 1).reshape(1024, 64), key_value_pages,
    )
    return res


def solution(mesh):
    in_specs = (
        P("group", None, "tensor"),
        P(None, "tensor"),
        P(None, "tensor"),
        P(None, "tensor"),
        P("tensor", None),
        P(None, "tensor", None),
        P(None, None, "tensor"),
        P(None, None, "tensor"),
        P(("group", "tensor"), None, None),
        P("group"),
        P("group"),
        P(),
        P(),
    )
    out_specs = P("group", None, "tensor")
    return jax.shard_map(local, mesh=mesh, in_specs=in_specs, out_specs=out_specs, check_vma=False)
```

```python
import functools
import math

import jax
import jax.numpy as jnp
import numpy as np
from jax import lax
from jax.experimental import pallas as pl
from jax.experimental.pallas import tpu as pltpu
from jax.sharding import PartitionSpec as P

QUERY_HEADS = 64
KEY_VALUE_HEADS = 8
HEAD_SIZE = 128
RANK_LIMIT = 64
ADAPTERS = 32
STEPS = 2
RES = 4
ROWS_DEV = 8
TOKENS = 512
POOL = 32
ROPE_BASE = 500000.0
MESH = pl.DeviceIdType.MESH
F32 = jnp.float32
BF16 = jnp.bfloat16


def dot(a, b):
    return jnp.dot(a, b, preferred_element_type=F32)


def dot_nt(a, b):
    return lax.dot_general(a, b, (((1,), (1,)), ((), ())), preferred_element_type=F32)


def dot_tn(a, b):
    return lax.dot_general(a, b, (((0,), (0,)), ((), ())), preferred_element_type=F32)


def remote(src, dst, send, recv, device):
    return pltpu.make_async_remote_copy(
        src_ref=src, dst_ref=dst, send_sem=send, recv_sem=recv,
        device_id=device, device_id_type=MESH,
    )


def kernel(
    hid, adapters, buckets, table_v, cos_tab, sin_tab, lengths, table,
    qw, kt, vt, ow, down, upq, upv, pool,
    out,
    hb, wq, wqp, kvt, wo, pages, dn, uq, uv,
    cos_t, sin_t, lens, pids, back,
    acc, metap, lowsend, lowrecv, scown, screcv, lift, liftv,
    send1, recv1, qs, kvs, knf, vnf, att, send2, recv2, lhs,
    sb, rh, rf, ta, ta0, rah, raf, kvperm,
    loc, ags, agr, wxs, wxr, fws, fwr, lows, lowr, scs, scr, s1s, s1r, s2s, s2r, rss, rsr, plane_sem, all_sem,
):
    g = lax.axis_index("group")
    t = lax.axis_index("tensor")
    core = g % 2
    z = t // 16
    y = (t // 4) % 4
    x = t % 4
    zp = 1 - z
    tp = zp * 16 + y * 4 + x
    g2 = (g + 2) % 4
    gs = g + 1 - 2 * core

    def near(along_b, d):
        on_x = (1 - core) * (1 - along_b) + core * along_b
        on_y = 1 - on_x
        xx = (x + 4 + d * on_x) % 4
        yy = (y + 4 + d * on_y) % 4
        return (g, z * 16 + yy * 4 + xx)

    def slice_index(oa, ob):
        dx = oa * (1 - core) + ob * core
        dy = oa * core + ob * (1 - core)
        return ((y + dy) % 4) * 4 + (x + dx) % 4

    half = z * 4096
    local = [
        (qw.at[pl.ds(pl.multiple_of(half, 4096), 4096)], wq),
        (kt.at[:, pl.ds(pl.multiple_of(half, 4096), 4096)], kvt.at[pl.ds(pl.multiple_of(z * 64, 32), 32)]),
        (vt.at[:, pl.ds(pl.multiple_of(half, 4096), 4096)], kvt.at[pl.ds(pl.multiple_of(z * 64 + 32, 32), 32)]),
        (ow.at[:, pl.ds(pl.multiple_of(half, 4096), 4096)], wo.at[z]),
        (down, dn),
        (upq, uq),
        (upv, uv),
        (pool, pages),
    ]
    local = [pltpu.make_async_copy(s, d, loc.at[i]) for i, (s, d) in enumerate(local)]
    for i in (4, 0, 1, 2, 5, 6, 3, 7):
        local[i].start()

    barrier = pltpu.get_barrier_semaphore()

    def ring_x(d):
        return (g, z * 16 + y * 4 + (x + d) % 4)

    def ring_y(d):
        return (g, z * 16 + ((y + d) % 4) * 4 + x)

    def line_z(d):
        zz = (2 * (g // 2) + z + d // 2) % 4
        return ((zz // 2) * 2 + (core + d) % 2, (zz % 2) * 16 + y * 4 + x)

    def greet(sem, device):
        pl.semaphore_signal(sem, inc=1, device_id=device, device_id_type=MESH)

    for d in range(1, 4):
        greet(barrier, ring_x(d))
        greet(barrier, ring_y(d))
    for d in range(1, 8):
        greet(barrier, line_z(d))

    def iota(shape, dim):
        return lax.broadcasted_iota(jnp.int32, shape, dim)

    tok = iota((8, TOKENS), 1)
    spread = (iota((256, TOKENS), 0) == iota((256, TOKENS), 1) // 2).astype(BF16)
    ahead = (
        (iota((256, TOKENS), 0) // 8 == iota((256, TOKENS), 1) // 16)
        & (iota((256, TOKENS), 0) < iota((256, TOKENS), 1) // 2)
    ).astype(BF16)
    first_page = table_v[0:1, pl.ds(pl.multiple_of(g * 256, 256), 256)]
    moved = (first_page // POOL != g * 32 + iota((1, 256), 1) // 8).astype(F32)
    moved = jnp.broadcast_to(moved, (8, 256)).astype(BF16)
    resumed = dot(moved, spread).astype(jnp.int32)
    before = dot(moved, ahead).astype(jnp.int32)
    place = jnp.where(resumed == 1, before, (tok // 2) % 8 - before)
    pos = (1 - resumed) * 256 + (tok // 16) * 8 + place * 2 + tok % 2
    perm = (iota((TOKENS, TOKENS), 0) == pos[0:1]).astype(BF16)
    mine = dot(perm, hid[...].reshape(TOKENS, 256)).astype(BF16)
    for h in range(2):
        hb[h, 0, 0] = mine[h * 256:(h + 1) * 256]

    def ag_copy(h, row, kind):
        along_b = 1 if row else 0
        oa = row - 1

        def at(o, rows=None):
            ref = hb.at[h, oa, o] if along_b else hb.at[h, o, 0]
            return ref if rows is None else ref.at[pl.ds(rows, 128)]

        if kind == 0:
            src, dst, d = at(0), at(1), -1
        elif kind == 1:
            src, dst, d = at(0), at(3), 1
        elif kind == 2:
            src, dst, d = at(1, 0), at(2, 0), -1
        else:
            src, dst, d = at(3, 128), at(2, 128), 1
        return remote(src, dst, ags.at[h, row, kind], agr.at[h, row, kind], near(along_b, d))

    ag = [[[ag_copy(h, row, kind) for kind in range(4)] for row in range(5)] for h in range(2)]

    def arrive(h, row, kind):
        ag[h][row][kind].wait_recv()

    def own(h):
        for row in (0, 1):
            for kind in (0, 1):
                ag[h][row][kind].start()

    def first_ring(h):
        arrive(h, 0, 0)
        ag[h][0][2].start()
        ag[h][2][0].start()
        ag[h][2][1].start()
        arrive(h, 0, 1)
        ag[h][0][3].start()
        ag[h][4][0].start()
        ag[h][4][1].start()
        forward(h, 0)

    def forward(h, oa):
        for kind in (0, 1):
            arrive(h, 1 + oa, kind)
            ag[h][1 + oa][kind + 2].start()

    def first_ring_far(h):
        arrive(h, 0, 2)
        arrive(h, 0, 3)
        ag[h][3][0].start()
        ag[h][3][1].start()

    def along(row):
        wide = jnp.broadcast_to(row.astype(F32), (128, 256)).astype(BF16)
        return dot_nt(perm, dot(wide, spread).astype(BF16))

    metap[:, :128] = along(adapters[...])
    lane = iota((TOKENS, 128), 1)
    idxi = metap[:, :128].astype(jnp.int32)

    local[4].wait()

    def low_part(first, count):
        total = None
        for a in range(first, first + count, 2):
            maps = jnp.concatenate([dn[a], dn[a + 1]], axis=1)
            part = jnp.concatenate([dot(hb[h, 0, 0], maps) for h in range(2)], axis=0)
            part = jnp.where(idxi == a, part[:, :128], 0.0) + jnp.where(idxi == a + 1, part[:, 128:], 0.0)
            total = part if total is None else total + part
        return total

    low = low_part(0, ADAPTERS)
    for l in range(2):
        lowsend[:, l] = low[l * 256:(l + 1) * 256].reshape(32, 8, 128).astype(BF16)
    metap[:, 128:] = along(buckets[...])

    pl.semaphore_wait(barrier, 13)
    own(0)
    for d in range(1, 4):
        greet(plane_sem, ring_y(d))

    def wx_pieces(zq, q, zd):
        c0 = pl.multiple_of(zd * 4096 + q * 1024, 1024)
        d0 = pl.multiple_of(q * 1024, 1024)
        r0 = pl.multiple_of(q * 64, 64)
        return [
            (qw.at[pl.ds(c0, 1024)], wqp.at[pl.ds(d0, 1024)]),
            (kt.at[:, pl.ds(c0, 1024)], kvt.at[pl.ds(pl.multiple_of(zq * 64, 32), 32), pl.ds(d0, 1024)]),
            (vt.at[:, pl.ds(c0, 1024)], kvt.at[pl.ds(pl.multiple_of(zq * 64 + 32, 32), 32), pl.ds(d0, 1024)]),
            (ow.at[pl.ds(r0, 64), pl.ds(pl.multiple_of(zd * 4096, 4096), 4096)], wo.at[zq, pl.ds(r0, 64)]),
        ]

    def wx_copies(i):
        s, d = wx_pieces(z, g, zp)[i]
        return [remote(s, d, wxs.at[i, j], wxr.at[i, j], (gd, tp)) for j, gd in enumerate((g, g2))]

    def wx_arrivals(i):
        res = []
        for j, q in enumerate((g, g2)):
            s, d = wx_pieces(zp, q, z)[i]
            res.append(remote(s, d, wxs.at[i, j], wxr.at[i, j], (g, tp)))
        return res

    def fw_copies(i):
        res = []
        for j, q in enumerate((g, g2)):
            _, d = wx_pieces(zp, q, z)[i]
            res.append(remote(d, d, fws.at[i, j], fwr.at[i, j], (gs, t)))
        return res

    def fw_arrivals(i):
        res = []
        for j, q in enumerate((gs, (gs + 2) % 4)):
            _, d = wx_pieces(zp, q, z)[i]
            res.append(remote(d, d, fws.at[i, j], fwr.at[i, j], (gs, t)))
        return res

    for i in range(3):
        for c in wx_copies(i):
            c.start()
    own(1)

    def low_copy(o):
        d = (t + o) % 32
        return remote(lowsend.at[d], lowrecv.at[t], lows, lowr, (g, d))

    def low_start(o, carry):
        low_copy(o).start()
        return carry

    pl.semaphore_wait(plane_sem, 3)
    for d in range(1, 8):
        greet(all_sem, line_z(d))
    first_ring(0)
    pl.semaphore_wait(all_sem, 7)
    lax.fori_loop(1, 32, low_start, 0, unroll=8)
    lowrecv[t] = lowsend[t]
    first_ring(1)
    first_ring_far(0)
    forward(0, 1)
    forward(0, 3)

    remote(lowrecv.at[pl.ds(0, 31)], lowrecv.at[pl.ds(0, 31)], lows, lowr, (g, tp)).wait_recv()
    lane16 = lax.broadcasted_iota(jnp.int32, (8, 128), 1) % RANK_LIMIT
    for l in range(2):
        lowrank = jnp.sum(lowrecv[:, l].astype(F32), axis=0)
        bucket = metap[pl.ds(pl.multiple_of(l * 256 + t * 8, 8), 8), 128:]
        scaled = jnp.where(lane16.astype(F32) < bucket, lowrank * (0.5 * RANK_LIMIT) / bucket, 0.0)
        scown[l] = scaled.astype(BF16)

    def sc_copy(o):
        d = (t + o) % 32
        return remote(scown, screcv.at[t], scs, scr, (g, d))

    def sc_start(o, carry):
        sc_copy(o).start()
        return carry

    lax.fori_loop(1, 32, sc_start, 0, unroll=8)
    screcv[t] = scown[...]
    for c in wx_copies(3):
        c.start()

    first_ring_far(1)
    forward(0, 2)
    forward(1, 1)
    forward(1, 3)
    base = (g * 32 + t) * POOL
    for l in range(2):
        gg = (g + 3 + l) % 4
        first = gg * 256 + t * ROWS_DEV
        marks, spots = [], []
        count = jnp.int32(0)
        for k in range(ROWS_DEV):
            mark = jnp.where(table[0, first + k] // POOL != gg * 32 + t, 1, 0)
            marks.append(mark)
            spots.append(jnp.where(mark == 1, count, k - count))
            count = count + mark
        for i in range(RES):
            mine = [(marks[k] == 1 - l) & (spots[k] == i) for k in range(ROWS_DEV)]
            row = l * RES + i
            lens[row] = sum(jnp.where(mine[k], lengths[first + k], 0) for k in range(ROWS_DEV))
            for j in range(4):
                page = sum(jnp.where(mine[k], table[j, first + k], 0) for k in range(ROWS_DEV))
                pids[row, j] = jnp.clip(page - base, 0, POOL - 1)
            cos_t[2 * row:2 * row + 2, :] = cos_tab[pl.ds(lens[row], 2), :]
            sin_t[2 * row:2 * row + 2, :] = sin_tab[pl.ds(lens[row], 2), :]

    eye = (iota((TOKENS, TOKENS), 0) == iota((TOKENS, TOKENS), 1)).astype(BF16)
    back[...] = dot_nt(eye, perm).astype(BF16)
    i0 = iota((512, 512), 0)
    target = ((i0 // 32) % 2) * 256 + ((i0 // 64) % 2) * 128 + (i0 // 128) * 32 + i0 % 32
    kvperm[...] = (target == iota((512, 512), 1)).astype(BF16)

    for i in (0, 1, 2):
        local[i].wait()
        for a, c in zip(wx_arrivals(i), fw_copies(i)):
            a.wait_recv()
            c.start()
    forward(1, 2)

    remote(screcv.at[pl.ds(0, 31)], screcv.at[pl.ds(0, 31)], scs, scr, (g, tp)).wait_recv()
    local[5].wait()
    local[6].wait()
    sc = jnp.concatenate([screcv[:, l].astype(F32).reshape(256, 128) for l in range(2)], axis=0)
    swapped = pltpu.roll(sc, 64, 1)
    sq = jnp.where(lane < 64, sc, swapped)
    svk = jnp.where(lane < 64, swapped, 0.0).astype(BF16)[:, :64]
    lift[...] = jnp.zeros(lift.shape, F32)

    def lift_step(j, carry):
        two = [jnp.where(idxi == 4 * j + 2 * e + lane // 64, sq, 0.0).astype(BF16) for e in range(2)]
        lift[...] = lift[...] + dot(jnp.concatenate(two, axis=1), uq[pl.ds(pl.multiple_of(j * 256, 256), 256)])
        return carry

    lax.fori_loop(0, ADAPTERS // 4, lift_step, 0, unroll=2)
    liftv[...] = jnp.zeros(liftv.shape, F32)
    def liftv_step(j, carry):
        part = dot_nt(svk, uv[pl.ds(pl.multiple_of(j * 128, 128), 128)])
        liftv[...] = liftv[...] + jnp.where(idxi == 4 * j + lane // 32, part, 0.0)
        return carry

    lax.fori_loop(0, ADAPTERS // 4, liftv_step, 0, unroll=2)
    lv = liftv[...]
    lv = lv + pltpu.roll(lv, 64, 1)
    lv = lv + pltpu.roll(lv, 32, 1)
    place = lane // 32 == 2 * z + 1
    liftv[...] = jnp.where(place, lv, 0.0)
    for i in (0, 1, 2):
        for a in fw_arrivals(i):
            a.wait_recv()
    acc[...] = jnp.zeros(acc.shape, F32)

    def project(h, oa, ob):
        k0 = pl.multiple_of(slice_index(oa, ob) * 256, 256)
        x_in = hb[h, oa, ob]
        rows = slice(h * 256, (h + 1) * 256)
        acc[rows, 0:256] = acc[rows, 0:256] + dot(x_in, wq[pl.ds(k0, 256)])
        acc[rows, 256:512] = acc[rows, 256:512] + dot(x_in, wqp[pl.ds(k0, 256)])
        acc[rows, 512:640] = acc[rows, 512:640] + dot_nt(x_in, kvt[:, pl.ds(k0, 256)])


    def message(l, v, block):
        send1[l, :, block] = v.reshape(32, 8, 128).astype(BF16)

    def s1_copy(l, o):
        d = (t + o) % 32
        return remote(send1.at[l, d], recv1.at[l, t], s1s.at[l], s1r.at[l], ((g + 1 - l) % 4, d))

    def project_near(h):
        for oa in range(4):
            project(h, oa, 0)
        for oa in (0, 1, 3, 2):
            project(h, oa, 1)
            project(h, oa, 3)

    def project_far(h):
        for oa in (0, 1, 3, 2):
            arrive(h, 1 + oa, 2)
            arrive(h, 1 + oa, 3)
            project(h, oa, 2)

    def scatter_rows(l):
        rows = slice(l * 256, (l + 1) * 256)
        for j in range(2):
            message(l, acc[rows, j * 128:(j + 1) * 128] + lift[rows, j * 128:(j + 1) * 128], 2 * z + j)
            message(l, acc[rows, 256 + j * 128:256 + (j + 1) * 128], 2 * zp + j)
        message(l, acc[rows, 512:640] + liftv[rows, :], 4)

        def start(o, carry):
            s1_copy(l, o).start()
            return carry

        lax.fori_loop(1, 32, start, 0, unroll=8)
        if l == 1:
            recv1[1, t] = send1[1, t]
        else:
            s1_copy(0, 0).start()

    def rows_arrive(recv, send_sem, recv_sem, l):
        ref = recv.at[1, pl.ds(0, 31)] if l == 1 else recv.at[0]
        return remote(ref, ref, send_sem.at[l], recv_sem.at[l], (g, tp))

    head_of = iota((128, 128), 0) % 64
    cache_pos = iota((272, 128), 0)
    step = iota((272, 128), 1) // 64

    def attend(l):
        cos8 = cos_t[l * 8:(l + 1) * 8, :]
        sin8 = sin_t[l * 8:(l + 1) * 8, :]
        for yx in range(16):
            m = recv1[l, yx].astype(F32) + recv1[l, 16 + yx].astype(F32)
            m = m.astype(BF16).astype(F32)
            q = m[:4]
            q = q * cos8[None] + pltpu.roll(q, 64, 2) * sin8[None]
            for zj in range(4):
                head = (zj // 2) * 32 + yx * 2 + zj % 2
                r0 = l * 512 + head * 8
                qs[r0:r0 + 8, :] = q[zj].astype(BF16).astype(F32)
            yy, xx = yx // 4, yx % 4
            r0 = (l * 4 + yy) * 8
            kvs[r0:r0 + 8, xx * 128:(xx + 1) * 128] = m[4]
        kvp = dot(kvs[l * 32:(l + 1) * 32, :].astype(BF16), kvperm[...])
        for yy in range(4):
            r0 = yy * 8
            for zz in range(2):
                k = kvp[r0:r0 + 8, zz * 128:(zz + 1) * 128]
                k = k * cos8 + pltpu.roll(k, 64, 1) * sin8
                n = zz * 4 + yy
                knf[l, 0:8, n * 128:(n + 1) * 128] = k
                vnf[l, 0:8, n * 128:(n + 1) * 128] = kvp[r0:r0 + 8, 256 + zz * 128:256 + (zz + 1) * 128]
        knf[l, 8:16, :] = jnp.zeros((8, 1024), F32)
        vnf[l, 8:16, :] = jnp.zeros((8, 1024), F32)
        knew = knf[l].astype(BF16)
        vnew = vnf[l].astype(BF16)

        for ii in range(RES):
            i = l * RES + ii
            q = jnp.concatenate(
                [qs[pl.ds(l * 512 + 2 * ii + st, 64, stride=8), :] for st in range(2)], axis=0
            )
            bd = jnp.concatenate(
                [jnp.where(head_of // 8 == n, q, 0.0).astype(BF16) for n in range(8)], axis=1
            )
            keys = jnp.concatenate([pages[pids[i, j], :, :1024] for j in range(4)] + [knew], axis=0)
            values = jnp.concatenate([pages[pids[i, j], :, 1024:] for j in range(4)], axis=0)
            scores = dot_nt(keys, bd) * HEAD_SIZE ** (-0.5)
            first = 256 + 2 * ii
            usable = (
                (cache_pos < lens[i])
                | (cache_pos == first)
                | ((cache_pos == first + 1) & (step == 1))
            )
            top = jnp.max(jnp.where(usable, scores, -jnp.inf), axis=0, keepdims=True)
            e = jnp.where(usable, jnp.exp(scores - top), 0.0)
            probs = (e / jnp.sum(e, axis=0, keepdims=True)).astype(BF16)
            o = dot_tn(probs[:256], values) + dot_tn(probs[256:], vnew)
            for st in range(2):
                for n in range(8):
                    r0 = (2 * i + st) * 64 + n * 8
                    att[r0:r0 + 8, :] = o[st * 64 + n * 8:st * 64 + (n + 1) * 8, n * 128:(n + 1) * 128]

        def pack(yx, carry):
            for zj in range(4):
                head = (zj // 2) * 32 + yx * 2 + zj % 2
                send2[l, yx, zj] = att[pl.ds(l * 512 + head, 8, stride=64), :].astype(BF16)
            return carry

        lax.fori_loop(0, 16, pack, 0, unroll=4)

    def s2_copy(l, o):
        d = (t + o) % 32
        return remote(send2.at[l, d % 16], recv2.at[l, t], s2s.at[l], s2r.at[l], ((g + 3 + l) % 4, d))

    def scatter_heads(l):
        def start(o, carry):
            s2_copy(l, o).start()
            return carry

        lax.fori_loop(1, 32, start, 0, unroll=8)
        if l == 1:
            recv2[1, t] = send2[1, t % 16]
        else:
            s2_copy(0, 0).start()

    def build(l):
        rows_arrive(recv2, s2s, s2r, l).wait_recv()

        def some(k, carry):
            r0 = pl.multiple_of(l * 256 + k * 16, 16)
            for zj in range(4):
                both = jnp.concatenate([recv2[l, 2 * k + e, zj].astype(F32) for e in range(2)], axis=0)
                lhs[pl.ds(r0, 16), zj * 128:(zj + 1) * 128] = both.astype(BF16)
            return carry

        lax.fori_loop(0, 16, some, 0, unroll=4)

    def partial(h, oa, ob):
        c0 = pl.multiple_of(slice_index(oa, ob) * 256, 256)
        rows = slice(h * 256, (h + 1) * 256)
        return dot(lhs[rows, :256], wo[0, :, pl.ds(c0, 256)]) + dot(lhs[rows, 256:], wo[1, :, pl.ds(c0, 256)])

    def rs_copy(h, row, kind):
        along_b = 1 if row else 0
        oa = row - 1

        def src(o, rows=None):
            ref = sb.at[h, oa, o] if along_b else ta.at[h, o]
            return ref if rows is None else ref.at[pl.ds(rows, 128)]

        halves = rh.at[h, oa] if along_b else rah.at[h]
        fulls = rf.at[h, oa] if along_b else raf.at[h]
        if kind == 0:
            s, d, way = src(2, 0), halves.at[0], -1
        elif kind == 1:
            s, d, way = src(2, 128), halves.at[1], 1
        elif kind == 2:
            s, d, way = src(3), fulls.at[0], -1
        else:
            s, d, way = src(1), fulls.at[1], 1
        return remote(s, d, rss.at[h, row, kind], rsr.at[h, row, kind], near(along_b, way))

    rs = [[[rs_copy(h, row, kind) for kind in range(4)] for row in range(5)] for h in range(2)]
    order = (2, 1, 3, 0)

    def reduce_far(h):
        for oa in order:
            sb[h, oa, 2] = partial(h, oa, 2).astype(BF16)
            rs[h][1 + oa][0].start()
            rs[h][1 + oa][1].start()

    def reduce_near(h):
        for oa in order:
            part = partial(h, oa, 3)
            rs[h][1 + oa][0].wait_recv()
            sb[h, oa, 3, 0:128] = (part[0:128] + rh[h, oa, 0].astype(F32)).astype(BF16)
            sb[h, oa, 3, 128:256] = part[128:256].astype(BF16)
            rs[h][1 + oa][2].start()
            part = partial(h, oa, 1)
            rs[h][1 + oa][1].wait_recv()
            sb[h, oa, 1, 0:128] = part[0:128].astype(BF16)
            sb[h, oa, 1, 128:256] = (part[128:256] + rh[h, oa, 1].astype(F32)).astype(BF16)
            rs[h][1 + oa][3].start()

    def total(h, oa):
        part = partial(h, oa, 0)
        rs[h][1 + oa][2].wait_recv()
        rs[h][1 + oa][3].wait_recv()
        return part + rf[h, oa, 0].astype(F32) + rf[h, oa, 1].astype(F32)

    def reduce_first(h):
        ta[h, 2] = total(h, 2).astype(BF16)
        rs[h][0][0].start()
        rs[h][0][1].start()

    def reduce_last(h):
        part = total(h, 1)
        rs[h][0][1].wait_recv()
        ta[h, 1, 0:128] = part[0:128].astype(BF16)
        ta[h, 1, 128:256] = (part[128:256] + rah[h, 1].astype(F32)).astype(BF16)
        rs[h][0][3].start()
        part = total(h, 3)
        rs[h][0][0].wait_recv()
        ta[h, 3, 0:128] = (part[0:128] + rah[h, 0].astype(F32)).astype(BF16)
        ta[h, 3, 128:256] = part[128:256].astype(BF16)
        rs[h][0][2].start()
        ta0[h] = total(h, 0)

    def result(h):
        rs[h][0][2].wait_recv()
        rs[h][0][3].wait_recv()
        return (ta0[h] + raf[h, 0].astype(F32) + raf[h, 1].astype(F32)).astype(BF16)

    project_near(0)
    project_far(0)
    scatter_rows(0)
    project_near(1)
    project_far(1)
    scatter_rows(1)
    local[7].wait()
    rows_arrive(recv1, s1s, s1r, 0).wait_recv()
    attend(0)
    scatter_heads(0)
    local[3].wait()
    for a, c in zip(wx_arrivals(3), fw_copies(3)):
        a.wait_recv()
        c.start()
    rows_arrive(recv1, s1s, s1r, 1).wait_recv()
    attend(1)
    scatter_heads(1)
    for a in fw_arrivals(3):
        a.wait_recv()
    build(0)
    reduce_far(0)
    reduce_near(0)
    build(1)
    reduce_far(1)
    reduce_first(0)
    reduce_near(1)
    reduce_last(0)
    reduce_first(1)
    reduce_last(1)
    low_half = result(0)
    final = jnp.concatenate([low_half, result(1)], axis=0)
    out[...] = dot(back[...], final).astype(BF16).reshape(256, STEPS, 256)

    for h in range(2):
        for row in range(5):
            for kind in range(4):
                ag[h][row][kind].wait_send()
                rs[h][row][kind].wait_send()
    for i in range(4):
        for c in wx_copies(i) + fw_copies(i):
            c.wait_send()
    remote(lowrecv.at[pl.ds(0, 31)], lowrecv.at[pl.ds(0, 31)], lows, lowr, (g, tp)).wait_send()
    remote(screcv.at[pl.ds(0, 31)], screcv.at[pl.ds(0, 31)], scs, scr, (g, tp)).wait_send()
    for l in range(2):
        rows_arrive(recv1, s1s, s1r, l).wait_send()
        rows_arrive(recv2, s2s, s2r, l).wait_send()


def scratch():
    v = pltpu.VMEM
    dma = pltpu.SemaphoreType.DMA
    return [
        v((2, 4, 4, 256, 256), BF16),
        v((4096, 256), BF16),
        v((4096, 256), BF16),
        v((128, 4096), BF16),
        v((2, 256, 4096), BF16),
        v((32, 64, 2048), BF16),
        v((32, 256, 128), BF16),
        v((2048, 256), BF16),
        v((1024, 64), BF16),
        v((16, 128), F32),
        v((16, 128), F32),
        pltpu.SMEM((8,), jnp.int32),
        pltpu.SMEM((8, 4), jnp.int32),
        v((512, 512), BF16),
        v((512, 640), F32),
        v((512, 256), F32),
        v((32, 2, 8, 128), BF16),
        v((32, 2, 8, 128), BF16),
        v((2, 8, 128), BF16),
        v((32, 2, 8, 128), BF16),
        v((512, 256), F32),
        v((512, 128), F32),
        v((2, 32, 5, 8, 128), BF16),
        v((2, 32, 5, 8, 128), BF16),
        v((1024, 128), F32),
        v((64, 512), F32),
        v((2, 16, 1024), F32),
        v((2, 16, 1024), F32),
        v((1024, 128), F32),
        v((2, 16, 4, 8, 128), BF16),
        v((2, 32, 4, 8, 128), BF16),
        v((512, 512), BF16),
        v((2, 4, 4, 256, 256), BF16),
        v((2, 4, 2, 128, 256), BF16),
        v((2, 4, 2, 256, 256), BF16),
        v((2, 4, 256, 256), BF16),
        v((2, 256, 256), F32),
        v((2, 2, 128, 256), BF16),
        v((2, 2, 256, 256), BF16),
        v((512, 512), BF16),
        dma((8,)),
        dma((2, 5, 4)), dma((2, 5, 4)),
        dma((4, 2)), dma((4, 2)),
        dma((4, 2)), dma((4, 2)),
        dma, dma, dma, dma,
        dma((2,)), dma((2,)),
        dma((2,)), dma((2,)),
        dma((2, 5, 4)), dma((2, 5, 4)),
        pltpu.SemaphoreType.REGULAR,
        pltpu.SemaphoreType.REGULAR,
    ]


def local(
    hidden, query_weight, key_weight, value_weight, output_weight, adapter_down_maps,
    adapter_up_query, adapter_up_value, key_value_pages, row_adapter_index,
    row_rank_bucket, lengths, row_page_index,
):
    positions = np.arange(264, dtype=np.float32)
    inverse_freq = np.exp(np.float32(-math.log(ROPE_BASE)) * np.arange(64, dtype=np.float32) / np.float32(64))
    angles = positions[:, None] * np.concatenate([inverse_freq, inverse_freq])[None].astype(np.float32)
    sign = np.where(np.arange(128) < 64, -1.0, 1.0)[None]
    cos_tab = jnp.asarray(np.cos(angles), F32)
    sin_tab = jnp.asarray(np.sin(angles) * sign, F32)

    vm = pl.BlockSpec(memory_space=pltpu.VMEM)
    sm = pl.BlockSpec(memory_space=pltpu.SMEM)
    hbm = pl.BlockSpec(memory_space=pl.ANY)
    res = pl.pallas_call(
        kernel,
        out_shape=jax.ShapeDtypeStruct((256, STEPS, 256), BF16),
        in_specs=[vm] * 6 + [sm] * 2 + [hbm] * 8,
        out_specs=vm,
        scratch_shapes=scratch(),
        compiler_params=pltpu.CompilerParams(
            collective_id=0, has_side_effects=True, vmem_limit_bytes=60 * 1024 * 1024
        ),
    )(
        hidden, row_adapter_index[None, :], row_rank_bucket[None, :], row_page_index.T,
        cos_tab, sin_tab, lengths, row_page_index.T,
        query_weight, key_weight.T, value_weight.T, output_weight, adapter_down_maps,
        adapter_up_query.reshape(2048, 256),
        adapter_up_value.transpose(0, 2, 1).reshape(1024, 64), key_value_pages,
    )
    return res


def solution(mesh):
    in_specs = (
        P("group", None, "tensor"),
        P(None, "tensor"),
        P(None, "tensor"),
        P(None, "tensor"),
        P("tensor", None),
        P(None, "tensor", None),
        P(None, None, "tensor"),
        P(None, None, "tensor"),
        P(("group", "tensor"), None, None),
        P("group"),
        P("group"),
        P(),
        P(),
    )
    out_specs = P("group", None, "tensor")
    return jax.shard_map(local, mesh=mesh, in_specs=in_specs, out_specs=out_specs, check_vma=False)
```

```python
import functools
import math

import jax
import jax.numpy as jnp
import numpy as np
from jax import lax
from jax.experimental import pallas as pl
from jax.experimental.pallas import tpu as pltpu
from jax.sharding import PartitionSpec as P

QUERY_HEADS = 64
KEY_VALUE_HEADS = 8
HEAD_SIZE = 128
RANK_LIMIT = 64
ADAPTERS = 32
STEPS = 2
RES = 4
ROWS_DEV = 8
TOKENS = 512
POOL = 32
ROPE_BASE = 500000.0
MESH = pl.DeviceIdType.MESH
F32 = jnp.float32
BF16 = jnp.bfloat16


def dot(a, b):
    return jnp.dot(a, b, preferred_element_type=F32)


def dot_nt(a, b):
    return lax.dot_general(a, b, (((1,), (1,)), ((), ())), preferred_element_type=F32)


def dot_tn(a, b):
    return lax.dot_general(a, b, (((0,), (0,)), ((), ())), preferred_element_type=F32)


def remote(src, dst, send, recv, device):
    return pltpu.make_async_remote_copy(
        src_ref=src, dst_ref=dst, send_sem=send, recv_sem=recv,
        device_id=device, device_id_type=MESH,
    )


def kernel(
    hid, adapters, buckets, table_v, cos_tab, sin_tab, lengths, table,
    qw, kt, vt, ow, down, upq, upv, pool,
    out,
    hb, wq, wqp, kvt, wo, pages, dn, uq, uv,
    cos_t, sin_t, lens, pids, back,
    acc, metap, lowsend, lowrecv, scown, screcv, lift, liftv,
    send1, recv1, qs, kvs, knf, vnf, att, send2, recv2, lhs,
    sb, rh, rf, ta, ta0, rah, raf, kvperm,
    loc, ags, agr, wxs, wxr, fws, fwr, lows, lowr, scs, scr, s1s, s1r, s2s, s2r, rss, rsr, plane_sem, all_sem,
):
    g = lax.axis_index("group")
    t = lax.axis_index("tensor")
    core = g % 2
    z = t // 16
    y = (t // 4) % 4
    x = t % 4
    zp = 1 - z
    tp = zp * 16 + y * 4 + x
    g2 = (g + 2) % 4
    gs = g + 1 - 2 * core

    def near(along_b, d):
        on_x = (1 - core) * (1 - along_b) + core * along_b
        on_y = 1 - on_x
        xx = (x + 4 + d * on_x) % 4
        yy = (y + 4 + d * on_y) % 4
        return (g, z * 16 + yy * 4 + xx)

    def slice_index(oa, ob):
        dx = oa * (1 - core) + ob * core
        dy = oa * core + ob * (1 - core)
        return ((y + dy) % 4) * 4 + (x + dx) % 4

    half = z * 4096
    local = [
        (qw.at[pl.ds(pl.multiple_of(half, 4096), 4096)], wq),
        (kt.at[:, pl.ds(pl.multiple_of(half, 4096), 4096)], kvt.at[pl.ds(pl.multiple_of(z * 64, 32), 32)]),
        (vt.at[:, pl.ds(pl.multiple_of(half, 4096), 4096)], kvt.at[pl.ds(pl.multiple_of(z * 64 + 32, 32), 32)]),
        (ow.at[:, pl.ds(pl.multiple_of(half, 4096), 4096)], wo.at[z]),
        (down, dn),
        (upq, uq),
        (upv, uv),
        (pool, pages),
    ]
    local = [pltpu.make_async_copy(s, d, loc.at[i]) for i, (s, d) in enumerate(local)]
    for i in (4, 0, 1, 2, 5, 6, 3, 7):
        local[i].start()

    barrier = pltpu.get_barrier_semaphore()

    def ring_x(d):
        return (g, z * 16 + y * 4 + (x + d) % 4)

    def ring_y(d):
        return (g, z * 16 + ((y + d) % 4) * 4 + x)

    def line_z(d):
        zz = (2 * (g // 2) + z + d // 2) % 4
        return ((zz // 2) * 2 + (core + d) % 2, (zz % 2) * 16 + y * 4 + x)

    def greet(sem, device):
        pl.semaphore_signal(sem, inc=1, device_id=device, device_id_type=MESH)

    for d in range(1, 4):
        greet(barrier, ring_x(d))
        greet(barrier, ring_y(d))
    for d in range(1, 8):
        greet(barrier, line_z(d))

    def iota(shape, dim):
        return lax.broadcasted_iota(jnp.int32, shape, dim)

    tok = iota((8, TOKENS), 1)
    spread = (iota((256, TOKENS), 0) == iota((256, TOKENS), 1) // 2).astype(BF16)
    ahead = (
        (iota((256, TOKENS), 0) // 8 == iota((256, TOKENS), 1) // 16)
        & (iota((256, TOKENS), 0) < iota((256, TOKENS), 1) // 2)
    ).astype(BF16)
    first_page = table_v[0:1, pl.ds(pl.multiple_of(g * 256, 256), 256)]
    moved = (first_page // POOL != g * 32 + iota((1, 256), 1) // 8).astype(F32)
    moved = jnp.broadcast_to(moved, (8, 256)).astype(BF16)
    resumed = dot(moved, spread).astype(jnp.int32)
    before = dot(moved, ahead).astype(jnp.int32)
    place = jnp.where(resumed == 1, before, (tok // 2) % 8 - before)
    pos = (1 - resumed) * 256 + (tok // 16) * 8 + place * 2 + tok % 2
    perm = (iota((TOKENS, TOKENS), 0) == pos[0:1]).astype(BF16)
    mine = dot(perm, hid[...].reshape(TOKENS, 256)).astype(BF16)
    for h in range(2):
        hb[h, 0, 0] = mine[h * 256:(h + 1) * 256]

    def ag_copy(h, row, kind):
        along_b = 1 if row else 0
        oa = row - 1

        def at(o, rows=None):
            ref = hb.at[h, oa, o] if along_b else hb.at[h, o, 0]
            return ref if rows is None else ref.at[pl.ds(rows, 128)]

        if kind == 0:
            src, dst, d = at(0), at(1), -1
        elif kind == 1:
            src, dst, d = at(0), at(3), 1
        elif kind == 2:
            src, dst, d = at(1, 0), at(2, 0), -1
        else:
            src, dst, d = at(3, 128), at(2, 128), 1
        return remote(src, dst, ags.at[h, row, kind], agr.at[h, row, kind], near(along_b, d))

    ag = [[[ag_copy(h, row, kind) for kind in range(4)] for row in range(5)] for h in range(2)]

    def arrive(h, row, kind):
        ag[h][row][kind].wait_recv()

    def own(h):
        for row in (0, 1):
            for kind in (0, 1):
                ag[h][row][kind].start()

    def first_ring(h):
        arrive(h, 0, 0)
        ag[h][0][2].start()
        ag[h][2][0].start()
        ag[h][2][1].start()
        arrive(h, 0, 1)
        ag[h][0][3].start()
        ag[h][4][0].start()
        ag[h][4][1].start()
        forward(h, 0)

    def forward(h, oa):
        for kind in (0, 1):
            arrive(h, 1 + oa, kind)
            ag[h][1 + oa][kind + 2].start()

    def first_ring_far(h):
        arrive(h, 0, 2)
        arrive(h, 0, 3)
        ag[h][3][0].start()
        ag[h][3][1].start()

    def along(row):
        wide = jnp.broadcast_to(row.astype(F32), (128, 256)).astype(BF16)
        return dot_nt(perm, dot(wide, spread).astype(BF16))

    metap[:, :128] = along(adapters[...])
    lane = iota((TOKENS, 128), 1)
    idxi = metap[:, :128].astype(jnp.int32)

    local[4].wait()

    def low_part(first, count):
        total = None
        for a in range(first, first + count, 2):
            maps = jnp.concatenate([dn[a], dn[a + 1]], axis=1)
            part = jnp.concatenate([dot(hb[h, 0, 0], maps) for h in range(2)], axis=0)
            part = jnp.where(idxi == a, part[:, :128], 0.0) + jnp.where(idxi == a + 1, part[:, 128:], 0.0)
            total = part if total is None else total + part
        return total

    low = low_part(0, ADAPTERS)
    for l in range(2):
        lowsend[:, l] = low[l * 256:(l + 1) * 256].reshape(32, 8, 128).astype(BF16)
    metap[:, 128:] = along(buckets[...])

    pl.semaphore_wait(barrier, 13)
    own(0)
    for d in range(1, 4):
        greet(plane_sem, ring_y(d))

    def wx_pieces(zq, q, zd):
        c0 = pl.multiple_of(zd * 4096 + q * 1024, 1024)
        d0 = pl.multiple_of(q * 1024, 1024)
        r0 = pl.multiple_of(q * 64, 64)
        return [
            (qw.at[pl.ds(c0, 1024)], wqp.at[pl.ds(d0, 1024)]),
            (kt.at[:, pl.ds(c0, 1024)], kvt.at[pl.ds(pl.multiple_of(zq * 64, 32), 32), pl.ds(d0, 1024)]),
            (vt.at[:, pl.ds(c0, 1024)], kvt.at[pl.ds(pl.multiple_of(zq * 64 + 32, 32), 32), pl.ds(d0, 1024)]),
            (ow.at[pl.ds(r0, 64), pl.ds(pl.multiple_of(zd * 4096, 4096), 4096)], wo.at[zq, pl.ds(r0, 64)]),
        ]

    def wx_copies(i):
        s, d = wx_pieces(z, g, zp)[i]
        return [remote(s, d, wxs.at[i, j], wxr.at[i, j], (gd, tp)) for j, gd in enumerate((g, g2))]

    def wx_arrivals(i):
        res = []
        for j, q in enumerate((g, g2)):
            s, d = wx_pieces(zp, q, z)[i]
            res.append(remote(s, d, wxs.at[i, j], wxr.at[i, j], (g, tp)))
        return res

    def fw_copies(i):
        res = []
        for j, q in enumerate((g, g2)):
            _, d = wx_pieces(zp, q, z)[i]
            res.append(remote(d, d, fws.at[i, j], fwr.at[i, j], (gs, t)))
        return res

    def fw_arrivals(i):
        res = []
        for j, q in enumerate((gs, (gs + 2) % 4)):
            _, d = wx_pieces(zp, q, z)[i]
            res.append(remote(d, d, fws.at[i, j], fwr.at[i, j], (gs, t)))
        return res

    for i in range(3):
        for c in wx_copies(i):
            c.start()
    own(1)

    def low_copy(o):
        d = (t + o) % 32
        return remote(lowsend.at[d], lowrecv.at[t], lows, lowr, (g, d))

    def low_start(o, carry):
        low_copy(o).start()
        return carry

    pl.semaphore_wait(plane_sem, 3)
    for d in range(1, 8):
        greet(all_sem, line_z(d))
    first_ring(0)
    pl.semaphore_wait(all_sem, 7)
    lax.fori_loop(1, 32, low_start, 0, unroll=8)
    lowrecv[t] = lowsend[t]
    first_ring(1)
    first_ring_far(0)
    forward(0, 1)
    forward(0, 3)

    remote(lowrecv.at[pl.ds(0, 31)], lowrecv.at[pl.ds(0, 31)], lows, lowr, (g, tp)).wait_recv()
    lane16 = lax.broadcasted_iota(jnp.int32, (8, 128), 1) % RANK_LIMIT
    for l in range(2):
        lowrank = jnp.sum(lowrecv[:, l].astype(F32), axis=0)
        bucket = metap[pl.ds(pl.multiple_of(l * 256 + t * 8, 8), 8), 128:]
        scaled = jnp.where(lane16.astype(F32) < bucket, lowrank * (0.5 * RANK_LIMIT) / bucket, 0.0)
        scown[l] = scaled.astype(BF16)

    def sc_copy(o):
        d = (t + o) % 32
        return remote(scown, screcv.at[t], scs, scr, (g, d))

    def sc_start(o, carry):
        sc_copy(o).start()
        return carry

    lax.fori_loop(1, 32, sc_start, 0, unroll=8)
    screcv[t] = scown[...]
    for c in wx_copies(3):
        c.start()

    first_ring_far(1)
    forward(0, 2)
    forward(1, 1)
    forward(1, 3)
    base = (g * 32 + t) * POOL
    for l in range(2):
        gg = (g + 3 + l) % 4
        first = gg * 256 + t * ROWS_DEV
        marks, spots = [], []
        count = jnp.int32(0)
        for k in range(ROWS_DEV):
            mark = jnp.where(table[0, first + k] // POOL != gg * 32 + t, 1, 0)
            marks.append(mark)
            spots.append(jnp.where(mark == 1, count, k - count))
            count = count + mark
        for i in range(RES):
            mine = [(marks[k] == 1 - l) & (spots[k] == i) for k in range(ROWS_DEV)]
            row = l * RES + i
            lens[row] = sum(jnp.where(mine[k], lengths[first + k], 0) for k in range(ROWS_DEV))
            for j in range(4):
                page = sum(jnp.where(mine[k], table[j, first + k], 0) for k in range(ROWS_DEV))
                pids[row, j] = jnp.clip(page - base, 0, POOL - 1)
            cos_t[2 * row:2 * row + 2, :] = cos_tab[pl.ds(lens[row], 2), :]
            sin_t[2 * row:2 * row + 2, :] = sin_tab[pl.ds(lens[row], 2), :]

    eye = (iota((TOKENS, TOKENS), 0) == iota((TOKENS, TOKENS), 1)).astype(BF16)
    back[...] = dot_nt(eye, perm).astype(BF16)
    i0 = iota((512, 512), 0)
    target = ((i0 // 32) % 2) * 256 + ((i0 // 64) % 2) * 128 + (i0 // 128) * 32 + i0 % 32
    kvperm[...] = (target == iota((512, 512), 1)).astype(BF16)

    forward(1, 2)

    for i in (0, 1, 2):
        local[i].wait()
        for a, c in zip(wx_arrivals(i), fw_copies(i)):
            a.wait_recv()
            c.start()

    remote(screcv.at[pl.ds(0, 31)], screcv.at[pl.ds(0, 31)], scs, scr, (g, tp)).wait_recv()
    local[5].wait()
    local[6].wait()
    sc = jnp.concatenate([screcv[:, l].astype(F32).reshape(256, 128) for l in range(2)], axis=0)
    swapped = pltpu.roll(sc, 64, 1)
    sq = jnp.where(lane < 64, sc, swapped)
    svk = jnp.where(lane < 64, swapped, 0.0).astype(BF16)[:, :64]
    lift[...] = jnp.zeros(lift.shape, F32)

    def lift_step(j, carry):
        two = [jnp.where(idxi == 4 * j + 2 * e + lane // 64, sq, 0.0).astype(BF16) for e in range(2)]
        lift[...] = lift[...] + dot(jnp.concatenate(two, axis=1), uq[pl.ds(pl.multiple_of(j * 256, 256), 256)])
        return carry

    lax.fori_loop(0, ADAPTERS // 4, lift_step, 0, unroll=2)
    liftv[...] = jnp.zeros(liftv.shape, F32)
    def liftv_step(j, carry):
        part = dot_nt(svk, uv[pl.ds(pl.multiple_of(j * 128, 128), 128)])
        liftv[...] = liftv[...] + jnp.where(idxi == 4 * j + lane // 32, part, 0.0)
        return carry

    lax.fori_loop(0, ADAPTERS // 4, liftv_step, 0, unroll=2)
    lv = liftv[...]
    lv = lv + pltpu.roll(lv, 64, 1)
    lv = lv + pltpu.roll(lv, 32, 1)
    place = lane // 32 == 2 * z + 1
    liftv[...] = jnp.where(place, lv, 0.0)
    for i in (0, 1, 2):
        for a in fw_arrivals(i):
            a.wait_recv()
    acc[...] = jnp.zeros(acc.shape, F32)

    def project(h, oa, ob):
        k0 = pl.multiple_of(slice_index(oa, ob) * 256, 256)
        x_in = hb[h, oa, ob]
        rows = slice(h * 256, (h + 1) * 256)
        acc[rows, 0:256] = acc[rows, 0:256] + dot(x_in, wq[pl.ds(k0, 256)])
        acc[rows, 256:512] = acc[rows, 256:512] + dot(x_in, wqp[pl.ds(k0, 256)])
        acc[rows, 512:640] = acc[rows, 512:640] + dot_nt(x_in, kvt[:, pl.ds(k0, 256)])


    def message(l, v, block):
        send1[l, :, block] = v.reshape(32, 8, 128).astype(BF16)

    def s1_copy(l, o):
        d = (t + o) % 32
        return remote(send1.at[l, d], recv1.at[l, t], s1s.at[l], s1r.at[l], ((g + 1 - l) % 4, d))

    def project_near(h):
        for oa in range(4):
            project(h, oa, 0)
        for oa in (0, 1, 3, 2):
            project(h, oa, 1)
            project(h, oa, 3)

    def project_far(h):
        for oa in (0, 1, 3, 2):
            arrive(h, 1 + oa, 2)
            arrive(h, 1 + oa, 3)
            project(h, oa, 2)

    def scatter_rows(l):
        rows = slice(l * 256, (l + 1) * 256)
        for j in range(2):
            message(l, acc[rows, j * 128:(j + 1) * 128] + lift[rows, j * 128:(j + 1) * 128], 2 * z + j)
            message(l, acc[rows, 256 + j * 128:256 + (j + 1) * 128], 2 * zp + j)
        message(l, acc[rows, 512:640] + liftv[rows, :], 4)

        def start(o, carry):
            s1_copy(l, o).start()
            return carry

        lax.fori_loop(1, 32, start, 0, unroll=8)
        if l == 1:
            recv1[1, t] = send1[1, t]
        else:
            s1_copy(0, 0).start()

    def rows_arrive(recv, send_sem, recv_sem, l):
        ref = recv.at[1, pl.ds(0, 31)] if l == 1 else recv.at[0]
        return remote(ref, ref, send_sem.at[l], recv_sem.at[l], (g, tp))

    head_of = iota((128, 128), 0) % 64
    cache_pos = iota((272, 128), 0)
    step = iota((272, 128), 1) // 64

    def attend(l):
        cos8 = cos_t[l * 8:(l + 1) * 8, :]
        sin8 = sin_t[l * 8:(l + 1) * 8, :]
        for yx in range(16):
            m = recv1[l, yx].astype(F32) + recv1[l, 16 + yx].astype(F32)
            m = m.astype(BF16).astype(F32)
            q = m[:4]
            q = q * cos8[None] + pltpu.roll(q, 64, 2) * sin8[None]
            for zj in range(4):
                head = (zj // 2) * 32 + yx * 2 + zj % 2
                r0 = l * 512 + head * 8
                qs[r0:r0 + 8, :] = q[zj].astype(BF16).astype(F32)
            yy, xx = yx // 4, yx % 4
            r0 = (l * 4 + yy) * 8
            kvs[r0:r0 + 8, xx * 128:(xx + 1) * 128] = m[4]
        kvp = dot(kvs[l * 32:(l + 1) * 32, :].astype(BF16), kvperm[...])
        for yy in range(4):
            r0 = yy * 8
            for zz in range(2):
                k = kvp[r0:r0 + 8, zz * 128:(zz + 1) * 128]
                k = k * cos8 + pltpu.roll(k, 64, 1) * sin8
                n = zz * 4 + yy
                knf[l, 0:8, n * 128:(n + 1) * 128] = k
                vnf[l, 0:8, n * 128:(n + 1) * 128] = kvp[r0:r0 + 8, 256 + zz * 128:256 + (zz + 1) * 128]
        knf[l, 8:16, :] = jnp.zeros((8, 1024), F32)
        vnf[l, 8:16, :] = jnp.zeros((8, 1024), F32)
        knew = knf[l].astype(BF16)
        vnew = vnf[l].astype(BF16)

        for ii in range(RES):
            i = l * RES + ii
            q = jnp.concatenate(
                [qs[pl.ds(l * 512 + 2 * ii + st, 64, stride=8), :] for st in range(2)], axis=0
            )
            bd = jnp.concatenate(
                [jnp.where(head_of // 8 == n, q, 0.0).astype(BF16) for n in range(8)], axis=1
            )
            keys = jnp.concatenate([pages[pids[i, j], :, :1024] for j in range(4)] + [knew], axis=0)
            values = jnp.concatenate([pages[pids[i, j], :, 1024:] for j in range(4)], axis=0)
            scores = dot_nt(keys, bd) * HEAD_SIZE ** (-0.5)
            first = 256 + 2 * ii
            usable = (
                (cache_pos < lens[i])
                | (cache_pos == first)
                | ((cache_pos == first + 1) & (step == 1))
            )
            top = jnp.max(jnp.where(usable, scores, -jnp.inf), axis=0, keepdims=True)
            e = jnp.where(usable, jnp.exp(scores - top), 0.0)
            probs = (e / jnp.sum(e, axis=0, keepdims=True)).astype(BF16)
            o = dot_tn(probs[:256], values) + dot_tn(probs[256:], vnew)
            for st in range(2):
                for n in range(8):
                    r0 = (2 * i + st) * 64 + n * 8
                    att[r0:r0 + 8, :] = o[st * 64 + n * 8:st * 64 + (n + 1) * 8, n * 128:(n + 1) * 128]

        def pack(yx, carry):
            for zj in range(4):
                head = (zj // 2) * 32 + yx * 2 + zj % 2
                send2[l, yx, zj] = att[pl.ds(l * 512 + head, 8, stride=64), :].astype(BF16)
            return carry

        lax.fori_loop(0, 16, pack, 0, unroll=4)

    def s2_copy(l, o):
        d = (t + o) % 32
        return remote(send2.at[l, d % 16], recv2.at[l, t], s2s.at[l], s2r.at[l], ((g + 3 + l) % 4, d))

    def scatter_heads(l):
        def start(o, carry):
            s2_copy(l, o).start()
            return carry

        lax.fori_loop(1, 32, start, 0, unroll=8)
        if l == 1:
            recv2[1, t] = send2[1, t % 16]
        else:
            s2_copy(0, 0).start()

    def build(l):
        rows_arrive(recv2, s2s, s2r, l).wait_recv()

        def some(k, carry):
            r0 = pl.multiple_of(l * 256 + k * 16, 16)
            for zj in range(4):
                both = jnp.concatenate([recv2[l, 2 * k + e, zj].astype(F32) for e in range(2)], axis=0)
                lhs[pl.ds(r0, 16), zj * 128:(zj + 1) * 128] = both.astype(BF16)
            return carry

        lax.fori_loop(0, 16, some, 0, unroll=4)

    def partial(h, oa, ob):
        c0 = pl.multiple_of(slice_index(oa, ob) * 256, 256)
        rows = slice(h * 256, (h + 1) * 256)
        return dot(lhs[rows, :256], wo[0, :, pl.ds(c0, 256)]) + dot(lhs[rows, 256:], wo[1, :, pl.ds(c0, 256)])

    def rs_copy(h, row, kind):
        along_b = 1 if row else 0
        oa = row - 1

        def src(o, rows=None):
            ref = sb.at[h, oa, o] if along_b else ta.at[h, o]
            return ref if rows is None else ref.at[pl.ds(rows, 128)]

        halves = rh.at[h, oa] if along_b else rah.at[h]
        fulls = rf.at[h, oa] if along_b else raf.at[h]
        if kind == 0:
            s, d, way = src(2, 0), halves.at[0], -1
        elif kind == 1:
            s, d, way = src(2, 128), halves.at[1], 1
        elif kind == 2:
            s, d, way = src(3), fulls.at[0], -1
        else:
            s, d, way = src(1), fulls.at[1], 1
        return remote(s, d, rss.at[h, row, kind], rsr.at[h, row, kind], near(along_b, way))

    rs = [[[rs_copy(h, row, kind) for kind in range(4)] for row in range(5)] for h in range(2)]
    order = (2, 1, 3, 0)

    def reduce_far(h):
        for oa in order:
            sb[h, oa, 2] = partial(h, oa, 2).astype(BF16)
            rs[h][1 + oa][0].start()
            rs[h][1 + oa][1].start()

    def reduce_near(h):
        for oa in order:
            part = partial(h, oa, 3)
            rs[h][1 + oa][0].wait_recv()
            sb[h, oa, 3, 0:128] = (part[0:128] + rh[h, oa, 0].astype(F32)).astype(BF16)
            sb[h, oa, 3, 128:256] = part[128:256].astype(BF16)
            rs[h][1 + oa][2].start()
            part = partial(h, oa, 1)
            rs[h][1 + oa][1].wait_recv()
            sb[h, oa, 1, 0:128] = part[0:128].astype(BF16)
            sb[h, oa, 1, 128:256] = (part[128:256] + rh[h, oa, 1].astype(F32)).astype(BF16)
            rs[h][1 + oa][3].start()

    def total(h, oa):
        part = partial(h, oa, 0)
        rs[h][1 + oa][2].wait_recv()
        rs[h][1 + oa][3].wait_recv()
        return part + rf[h, oa, 0].astype(F32) + rf[h, oa, 1].astype(F32)

    def reduce_first(h):
        ta[h, 2] = total(h, 2).astype(BF16)
        rs[h][0][0].start()
        rs[h][0][1].start()

    def reduce_last(h):
        part = total(h, 1)
        rs[h][0][1].wait_recv()
        ta[h, 1, 0:128] = part[0:128].astype(BF16)
        ta[h, 1, 128:256] = (part[128:256] + rah[h, 1].astype(F32)).astype(BF16)
        rs[h][0][3].start()
        part = total(h, 3)
        rs[h][0][0].wait_recv()
        ta[h, 3, 0:128] = (part[0:128] + rah[h, 0].astype(F32)).astype(BF16)
        ta[h, 3, 128:256] = part[128:256].astype(BF16)
        rs[h][0][2].start()
        ta0[h] = total(h, 0)

    def result(h):
        rs[h][0][2].wait_recv()
        rs[h][0][3].wait_recv()
        return (ta0[h] + raf[h, 0].astype(F32) + raf[h, 1].astype(F32)).astype(BF16)

    project_near(0)
    project_far(0)
    scatter_rows(0)
    project_near(1)
    project_far(1)
    scatter_rows(1)
    local[7].wait()
    rows_arrive(recv1, s1s, s1r, 0).wait_recv()
    attend(0)
    scatter_heads(0)
    local[3].wait()
    for a, c in zip(wx_arrivals(3), fw_copies(3)):
        a.wait_recv()
        c.start()
    rows_arrive(recv1, s1s, s1r, 1).wait_recv()
    attend(1)
    scatter_heads(1)
    for a in fw_arrivals(3):
        a.wait_recv()
    build(0)
    reduce_far(0)
    reduce_near(0)
    build(1)
    reduce_far(1)
    reduce_first(0)
    reduce_near(1)
    reduce_last(0)
    reduce_first(1)
    reduce_last(1)
    low_half = result(0)
    final = jnp.concatenate([low_half, result(1)], axis=0)
    out[...] = dot(back[...], final).astype(BF16).reshape(256, STEPS, 256)

    for h in range(2):
        for row in range(5):
            for kind in range(4):
                ag[h][row][kind].wait_send()
                rs[h][row][kind].wait_send()
    for i in range(4):
        for c in wx_copies(i) + fw_copies(i):
            c.wait_send()
    remote(lowrecv.at[pl.ds(0, 31)], lowrecv.at[pl.ds(0, 31)], lows, lowr, (g, tp)).wait_send()
    remote(screcv.at[pl.ds(0, 31)], screcv.at[pl.ds(0, 31)], scs, scr, (g, tp)).wait_send()
    for l in range(2):
        rows_arrive(recv1, s1s, s1r, l).wait_send()
        rows_arrive(recv2, s2s, s2r, l).wait_send()


def scratch():
    v = pltpu.VMEM
    dma = pltpu.SemaphoreType.DMA
    return [
        v((2, 4, 4, 256, 256), BF16),
        v((4096, 256), BF16),
        v((4096, 256), BF16),
        v((128, 4096), BF16),
        v((2, 256, 4096), BF16),
        v((32, 64, 2048), BF16),
        v((32, 256, 128), BF16),
        v((2048, 256), BF16),
        v((1024, 64), BF16),
        v((16, 128), F32),
        v((16, 128), F32),
        pltpu.SMEM((8,), jnp.int32),
        pltpu.SMEM((8, 4), jnp.int32),
        v((512, 512), BF16),
        v((512, 640), F32),
        v((512, 256), F32),
        v((32, 2, 8, 128), BF16),
        v((32, 2, 8, 128), BF16),
        v((2, 8, 128), BF16),
        v((32, 2, 8, 128), BF16),
        v((512, 256), F32),
        v((512, 128), F32),
        v((2, 32, 5, 8, 128), BF16),
        v((2, 32, 5, 8, 128), BF16),
        v((1024, 128), F32),
        v((64, 512), F32),
        v((2, 16, 1024), F32),
        v((2, 16, 1024), F32),
        v((1024, 128), F32),
        v((2, 16, 4, 8, 128), BF16),
        v((2, 32, 4, 8, 128), BF16),
        v((512, 512), BF16),
        v((2, 4, 4, 256, 256), BF16),
        v((2, 4, 2, 128, 256), BF16),
        v((2, 4, 2, 256, 256), BF16),
        v((2, 4, 256, 256), BF16),
        v((2, 256, 256), F32),
        v((2, 2, 128, 256), BF16),
        v((2, 2, 256, 256), BF16),
        v((512, 512), BF16),
        dma((8,)),
        dma((2, 5, 4)), dma((2, 5, 4)),
        dma((4, 2)), dma((4, 2)),
        dma((4, 2)), dma((4, 2)),
        dma, dma, dma, dma,
        dma((2,)), dma((2,)),
        dma((2,)), dma((2,)),
        dma((2, 5, 4)), dma((2, 5, 4)),
        pltpu.SemaphoreType.REGULAR,
        pltpu.SemaphoreType.REGULAR,
    ]


def local(
    hidden, query_weight, key_weight, value_weight, output_weight, adapter_down_maps,
    adapter_up_query, adapter_up_value, key_value_pages, row_adapter_index,
    row_rank_bucket, lengths, row_page_index,
):
    positions = np.arange(264, dtype=np.float32)
    inverse_freq = np.exp(np.float32(-math.log(ROPE_BASE)) * np.arange(64, dtype=np.float32) / np.float32(64))
    angles = positions[:, None] * np.concatenate([inverse_freq, inverse_freq])[None].astype(np.float32)
    sign = np.where(np.arange(128) < 64, -1.0, 1.0)[None]
    cos_tab = jnp.asarray(np.cos(angles), F32)
    sin_tab = jnp.asarray(np.sin(angles) * sign, F32)

    vm = pl.BlockSpec(memory_space=pltpu.VMEM)
    sm = pl.BlockSpec(memory_space=pltpu.SMEM)
    hbm = pl.BlockSpec(memory_space=pl.ANY)
    res = pl.pallas_call(
        kernel,
        out_shape=jax.ShapeDtypeStruct((256, STEPS, 256), BF16),
        in_specs=[vm] * 6 + [sm] * 2 + [hbm] * 8,
        out_specs=vm,
        scratch_shapes=scratch(),
        compiler_params=pltpu.CompilerParams(
            collective_id=0, has_side_effects=True, vmem_limit_bytes=60 * 1024 * 1024
        ),
    )(
        hidden, row_adapter_index[None, :], row_rank_bucket[None, :], row_page_index.T,
        cos_tab, sin_tab, lengths, row_page_index.T,
        query_weight, key_weight.T, value_weight.T, output_weight, adapter_down_maps,
        adapter_up_query.reshape(2048, 256),
        adapter_up_value.transpose(0, 2, 1).reshape(1024, 64), key_value_pages,
    )
    return res


def solution(mesh):
    in_specs = (
        P("group", None, "tensor"),
        P(None, "tensor"),
        P(None, "tensor"),
        P(None, "tensor"),
        P("tensor", None),
        P(None, "tensor", None),
        P(None, None, "tensor"),
        P(None, None, "tensor"),
        P(("group", "tensor"), None, None),
        P("group"),
        P("group"),
        P(),
        P(),
    )
    out_specs = P("group", None, "tensor")
    return jax.shard_map(local, mesh=mesh, in_specs=in_specs, out_specs=out_specs, check_vma=False)
```
